32 devices in a mesh: dp: 8 (over z, y), row: 2 (over core), col: 2 (over x).
Axes of the slice: x: 2, y: 2, z: 4, core: 2. Of those that a mesh axis runs over, the one named last changes fastest.
Arguments:
- hidden_in: bfloat16 [4096, 2, 512], P('dp', 'row', 'col'), may hold values from -6 to 6
- doc_lens: int32 [8, 4], P('dp'), may hold values from 0 to 512, as said below
- norm1_gain: float32 [2, 512], P('row', 'col'), may hold values from 0.1 to 1.9
- wqkv: bfloat16 [2, 512, 3, 2, 512], P(None, 'col', None, 'row'), may hold values from -0.1875 to 0.1875
- wout: bfloat16 [2, 512, 2, 512], P(None, 'col', 'row'), may hold values from -1 to 1
- norm2_gain: float32 [2, 512], P('row', 'col'), may hold values from 0.1 to 1.9
- wi: bfloat16 [2, 512, 2, 2, 1312], P(None, 'col', None, 'row'), may hold values from -0.1875 to 0.1875
- wo: bfloat16 [2, 1312, 2, 512], P(None, 'col', 'row'), may hold values from -0.15625 to 0.15625
- out_grad: bfloat16 [4096, 2, 512], P('dp', 'row', 'col'), may hold values from -6 to 6
Outputs:
- hidden_out: bfloat16 [4096, 2, 512], P('dp', 'row', 'col')
- grad_in: float32 [4096, 2, 512], P('dp', 'row', 'col')
- grad_norm1: float32 [2, 512], P('row', 'col')
- grad_wqkv: float32 [2, 512, 3, 2, 512], P(None, 'col', None, 'row')
- grad_wout: float32 [2, 512, 2, 512], P(None, 'col', 'row')
- grad_norm2: float32 [2, 512], P('row', 'col')
- grad_wi: float32 [2, 512, 2, 2, 1312], P(None, 'col', None, 'row')
- grad_wo: float32 [2, 1312, 2, 512], P(None, 'col', 'row')
The draws below stay inside these ranges and needn't reach their ends.
Inputs may be any that keep to these rules, and one draw needn't show every extreme that they name: `doc_lens`: row g lists, in order, the lengths of the sequences packed from slot 0 of data group g (a length may be 0); each row sums to at least 256 and at most 512, and in every draw one row is a single sequence of exactly 512 tokens.
All inputs are finite; a program needn't handle non-finite values.
Results may differ from the reference program's by a relative error of at most 0.024.
Values may be sent and summed in bfloat16 or wider, within the bound.
No kernel may reach another device: no remote copies, remote signals or barrier semaphores. Data moves between devices by JAX's collectives and lax.ppermute only.
A program may use at most 128 MiB of HBM per device.

```python
import math
import jax
import jax.numpy as jnp
from jax import lax

D = 1024
H = 16
HD = 64
FF = 2624
CAP = 512
DOCS = 4
TOKENS = 4096
N_DP = 8


def draw_doc_lens(key, part):
    key = jax.random.fold_in(key, 11)
    key_fill, key_cut, key_full = jax.random.split(key, 3)
    filled = jax.random.randint(key_fill, (N_DP, 1), CAP // 2, CAP + 1).astype(jnp.int32)
    cut_points = jnp.sort(jax.random.randint(key_cut, (N_DP, DOCS - 1), 0, CAP + 1), axis=1).astype(jnp.int32)
    cut_points = cut_points * filled // CAP
    bounds = jnp.concatenate([jnp.zeros((N_DP, 1), jnp.int32), cut_points, filled], axis=1)
    lengths = bounds[:, 1:] - bounds[:, :-1]
    chosen = jax.random.randint(key_full, (), 0, N_DP)
    single = jnp.concatenate([jnp.full((1, 1), CAP, jnp.int32), jnp.zeros((1, DOCS - 1), jnp.int32)], axis=1)
    return jnp.where(jnp.arange(N_DP)[:, None] == chosen, single, lengths).astype(jnp.int32)


def level_of(stream_key, dims, pieces, low, high):
    factor_of, own = 1.0, jax.random.fold_in(stream_key, 6)
    for dim, parts in pieces:
        heights = jnp.exp(jax.random.uniform(jax.random.fold_in(own, dim), (parts,), jnp.float32, low / len(pieces), high / len(pieces)))
        factor_of = factor_of * jnp.repeat(heights, dims[dim] // parts).reshape([-1 if axis == dim else 1 for axis in range(len(dims))])
    return factor_of


def bell_draw(key, shape, spread, most, cuts=(), kind=jnp.bfloat16):
    factor_of = level_of(key, shape, cuts, -0.22, 0.18) if cuts else 1.0
    entries = jax.random.normal(key, shape, jnp.float32) * spread * factor_of
    return jnp.minimum(jnp.maximum(entries, -most), most).astype(kind)


def setup_inputs(seed: int = 0) -> dict:
    streams_of = jax.random.split(jax.random.key(seed), 10)
    hidden_in = bell_draw(streams_of[0], (TOKENS, 2, D // 2), 1.0, 6.0, ((0, 8), (1, 2), (2, 2)))
    doc_lens = draw_doc_lens(jax.random.fold_in(streams_of[9], 71), 0)
    norm1_gain = jnp.clip(1.0 + 0.18 * jax.random.normal(streams_of[2], (2, D // 2), jnp.float32), 0.1, 1.9)
    wqkv = bell_draw(streams_of[3], (2, D // 2, 3, 2, D // 2), D ** -0.5, 0.1875, ((1, 2), (3, 2)))
    wout = bell_draw(streams_of[4], (2, D // 2, 2, D // 2), (D // 32) ** -0.5, 1.0, ((1, 2), (2, 2)))
    norm2_gain = jnp.clip(1.0 + 0.18 * jax.random.normal(streams_of[5], (2, D // 2), jnp.float32), 0.1, 1.9)
    wi = bell_draw(streams_of[6], (2, D // 2, 2, 2, FF // 2), D ** -0.5, 0.1875, ((1, 2), (3, 2)))
    wo = bell_draw(streams_of[7], (2, FF // 2, 2, D // 2), (FF // 2) ** -0.5, 0.15625, ((1, 2), (2, 2)))
    out_grad = bell_draw(streams_of[8], (TOKENS, 2, D // 2), 1.0, 6.0, ((0, 8), (1, 2), (2, 2)))
    return dict(hidden_in=hidden_in, doc_lens=doc_lens, norm1_gain=norm1_gain, wqkv=wqkv, wout=wout, norm2_gain=norm2_gain, wi=wi, wo=wo, out_grad=out_grad)


EPSILON = 1e-05
ROPE_BASE = 160000.0

@jax.custom_vjp
def low(v):
    return lax.optimization_barrier(v.astype(jnp.bfloat16)).astype(jnp.float32)

@jax.custom_vjp
def low_back(v):
    return v

def low_keep(v):
    return (low(v), None)

def low_pass(kept, grad):
    return (grad,)

def back_keep(v):
    return (v, None)

def back_low(kept, grad):
    return (low(grad),)
low.defvjp(low_keep, low_pass)
low_back.defvjp(back_keep, back_low)

def matmul(left, right):
    return jnp.dot(left, right, precision=lax.Precision.HIGHEST)

def layer_norm(values, gain):
    average = lax.optimization_barrier(jnp.mean(values, axis=-1, keepdims=True))
    centred = values - average
    variance = lax.optimization_barrier(jnp.mean(centred * centred, axis=-1, keepdims=True))
    return centred * lax.rsqrt(variance + EPSILON) * gain

def layout(lengths):
    places = jnp.arange(CAP, dtype=jnp.int32)
    doc_ends = jnp.cumsum(lengths).astype(jnp.int32)
    passed = doc_ends[None, :] <= places[:, None]
    segment = lax.optimization_barrier(jnp.sum(passed.astype(jnp.int32), axis=1)).astype(jnp.int32)
    doc_start = lax.optimization_barrier(jnp.sum(jnp.where(passed, lengths[None, :], 0), axis=1)).astype(jnp.int32)
    occupied = (places < doc_ends[-1]).astype(jnp.float32)
    return (segment, places - doc_start, occupied)

def rotary(position):
    frequency = jnp.exp(jnp.arange(HD // 2, dtype=jnp.float32) * (-2.0 * math.log(ROPE_BASE) / HD))
    angles = position.astype(jnp.float32)[:, None] * frequency[None, :]
    angles = jnp.concatenate([angles, angles], axis=1)
    return (jnp.cos(angles), jnp.sin(angles))

def rotate(values, cosine_table, sine_table):
    halfway = values.shape[-1] // 2
    turned = jnp.concatenate([-values[..., halfway:], values[..., :halfway]], axis=-1)
    return values * cosine_table[:, None, :] + turned * sine_table[:, None, :]

def attend_block(queries, segment_rows, keys_all, values_all, segment):
    scores = jnp.einsum('qhd,khd->hqk', queries, keys_all, precision=lax.Precision.HIGHEST) * HD ** (-0.5)
    scores = low_back(scores)
    same_doc = segment_rows[:, None] == segment[None, :]
    scores = jnp.where(same_doc[None], scores, -1e+30)
    probabilities = low(jax.nn.softmax(scores, axis=-1))
    return jnp.einsum('hqk,khd->qhd', probabilities, values_all, precision=lax.Precision.HIGHEST)

def attention(queries, keys_all, values_all, segment):
    block_rows = min(512, CAP)
    query_blocks = queries.reshape(CAP // block_rows, block_rows, H, HD)
    segment_blocks = segment.reshape(CAP // block_rows, block_rows)
    stepper = jax.checkpoint(attend_block)
    results = lax.map(lambda element: stepper(element[0], element[1], keys_all, values_all, segment), (query_blocks, segment_blocks))
    return results.reshape(CAP, H, HD)

def forward(tokens_row, gain_one, weight_qkv, weight_out, gain_two, weight_in, weight_down, segment, position):
    cosine_table, sine_table = rotary(position)
    normed = low(layer_norm(tokens_row, gain_one.reshape(D)))
    projected = low_back(matmul(normed, weight_qkv.reshape(D, 3 * D))).reshape(CAP, 3, H, HD)
    queries = low(rotate(projected[:, 0], cosine_table, sine_table))
    keys_all = low(rotate(projected[:, 1], cosine_table, sine_table))
    values_all = low(projected[:, 2])
    attended = low(low_back(attention(queries, keys_all, values_all, segment))).reshape(CAP, D)
    branch = low_back(matmul(attended, weight_out.reshape(D, D)))
    middle = tokens_row + branch
    normed_two = low(layer_norm(middle, gain_two.reshape(D)))
    gate_up = low_back(matmul(normed_two, weight_in.reshape(D, 2 * FF))).reshape(CAP, 2, FF)
    hidden = low(jax.nn.gelu(gate_up[:, 0], approximate=False) * gate_up[:, 1])
    return middle + low_back(matmul(hidden, weight_down.reshape(FF, D)))

def reference(hidden_in, doc_lens, norm1_gain, wqkv, wout, norm2_gain, wi, wo, out_grad):
    params = (norm1_gain.astype(jnp.float32), wqkv.astype(jnp.float32), wout.astype(jnp.float32), norm2_gain.astype(jnp.float32), wi.astype(jnp.float32), wo.astype(jnp.float32))
    inputs = hidden_in.astype(jnp.float32).reshape(N_DP, CAP, D)
    cotangent = out_grad.astype(jnp.float32).reshape(N_DP, CAP, D)

    def per_group(totals, element):
        tokens_row, grad_rows, lengths = element
        segment, position, occupied = layout(lengths)

        def forward_group(tokens_in, gain_one, weight_qkv, weight_out, gain_two, weight_in, weight_down):
            return forward(tokens_in, gain_one, weight_qkv, weight_out, gain_two, weight_in, weight_down, segment, position)
        result, pullback = jax.vjp(forward_group, tokens_row, params[0], params[1], params[2], params[3], params[4], params[5])
        gradients = pullback(grad_rows * occupied[:, None])
        totals = tuple((running + fresh for running, fresh in zip(totals, gradients[1:])))
        return (totals, (result, gradients[0]))
    start_sums = tuple((jnp.zeros(param.shape, jnp.float32) for param in params))
    totals, (results, backs) = lax.scan(per_group, start_sums, (inputs, cotangent, doc_lens))
    return (results.reshape(TOKENS, 2, D // 2).astype(jnp.bfloat16), backs.reshape(TOKENS, 2, D // 2), totals[0], totals[1], totals[2], totals[3], totals[4], totals[5])
```

```python
import math

import jax
import jax.numpy as jnp
from jax import lax
from jax.sharding import PartitionSpec as P

HD = 64
EPSILON = 1e-05
ROPE_BASE = 160000.0
F32 = jnp.float32
BF = jnp.bfloat16


def layout(lengths, capacity):
    places = jnp.arange(capacity, dtype=jnp.int32)
    doc_ends = jnp.cumsum(lengths)
    passed = doc_ends[None, :] <= places[:, None]
    segment = jnp.sum(passed.astype(jnp.int32), axis=1)
    doc_start = jnp.sum(jnp.where(passed, lengths[None, :], 0), axis=1)
    occupied = (places < doc_ends[-1]).astype(F32)
    return (segment, places - doc_start, occupied)


def rotary(position, head_size):
    frequency = jnp.exp(
        jnp.arange(head_size // 2, dtype=F32) * (-2.0 * math.log(ROPE_BASE) / head_size)
    )
    angles = position.astype(F32)[:, None] * frequency[None, :]
    angles = jnp.concatenate([angles, angles], axis=1)
    return (jnp.cos(angles), jnp.sin(angles))


def rotate(values, cosine_table, sine_table):
    halfway = values.shape[-1] // 2
    turned = jnp.concatenate([-values[..., halfway:], values[..., :halfway]], axis=-1)
    return values * cosine_table[:, None, :] + turned * sine_table[:, None, :]


def rotate_back(grads, cosine_table, sine_table):
    halfway = grads.shape[-1] // 2
    sined = grads * sine_table[:, None, :]
    turned = jnp.concatenate([sined[..., halfway:], -sined[..., :halfway]], axis=-1)
    return grads * cosine_table[:, None, :] + turned


def geglu(gate_part, up_part):
    return jax.nn.gelu(gate_part, approximate=False) * up_part


def swap(value, axis):
    return lax.ppermute(value, axis, [(0, 1), (1, 0)])


def dp_swap(value, bit):
    size = lax.axis_size("dp")
    return lax.ppermute(value, "dp", [(i, i ^ bit) for i in range(size)])


def ordered(index, mine, other, axis):
    return jnp.where(
        index == 0,
        jnp.concatenate([mine, other], axis),
        jnp.concatenate([other, mine], axis),
    )


def pick(value, index, parts, axis):
    size = value.shape[axis] // parts
    return lax.dynamic_slice_in_dim(value, index * size, size, axis)


def dot(left, right, dims):
    return lax.dot_general(left, right, (dims, ((), ())), preferred_element_type=F32)


NN = ((1,), (0,))
NT = ((1,), (1,))
TN = ((0,), (0,))


def norm_forward(values):
    mean = jnp.mean(values, axis=1, keepdims=True)
    centred = values - mean
    scale = lax.rsqrt(jnp.mean(centred * centred, axis=1, keepdims=True) + EPSILON)
    return (centred * scale, scale)


def norm_backward(grad, normal, scale, gain):
    hat = grad * gain
    correction = (
        hat
        - jnp.mean(hat, axis=1, keepdims=True)
        - normal * jnp.mean(hat * normal, axis=1, keepdims=True)
    )
    return (scale * correction, jnp.sum(grad * normal, axis=0))


def masked_scores(queries, keys_all, segment):
    scores = jnp.einsum("qhd,khd->hqk", queries, keys_all, preferred_element_type=F32)
    scores = scores * (queries.shape[2] ** (-0.5))
    return jnp.where((segment[:, None] == segment[None, :])[None], scores, -1e30)


def attend_forward(queries, keys_all, values_all, segment):
    scores = masked_scores(queries, keys_all, segment)
    peak = jnp.max(scores, axis=2, keepdims=True)
    raised = jnp.exp(scores - peak)
    denominator = jnp.sum(raised, axis=2, keepdims=True)
    probabilities = (raised / denominator).astype(BF)
    outputs = jnp.einsum("hqk,khd->qhd", probabilities, values_all, preferred_element_type=F32)
    return (outputs, peak + jnp.log(denominator))


def attend_backward(queries, keys_all, values_all, grad_attended, logsums, segment):
    factor = queries.shape[2] ** (-0.5)
    scores = masked_scores(queries, keys_all, segment)
    probs = jnp.exp(scores - logsums)
    grad_values = jnp.einsum(
        "hqk,qhd->khd", probs.astype(BF), grad_attended, preferred_element_type=F32
    )
    grad_probs = jnp.einsum("qhd,khd->hqk", grad_attended, values_all, preferred_element_type=F32)
    grad_scores = (
        probs * (grad_probs - jnp.sum(probs * grad_probs, axis=2, keepdims=True))
    ).astype(BF)
    grad_queries = factor * jnp.einsum(
        "hqk,khd->qhd", grad_scores, keys_all, preferred_element_type=F32
    )
    grad_keys = factor * jnp.einsum(
        "hqk,qhd->khd", grad_scores, queries, preferred_element_type=F32
    )
    return (grad_queries, grad_keys, grad_values)


def bits_of(size):
    assert size & (size - 1) == 0
    return [1 << k for k in range(size.bit_length() - 1)]


def dp_scatter(value, order, axis):
    index = lax.axis_index("dp")
    parts = [value]
    for bit in order:
        mine = (index // bit) % 2

        def side(which):
            total = None
            for part in parts:
                piece = pick(part, which, 2, axis).astype(F32)
                total = piece if total is None else total + piece
            return total.astype(BF)

        sent, kept = side(1 - mine), side(mine)
        parts = [kept, dp_swap(sent, bit)]
    return (parts[0].astype(F32) + parts[1].astype(F32)).astype(BF)


def dp_gather(value, order, axis):
    index = lax.axis_index("dp")
    for bit in reversed(order):
        mine = (index // bit) % 2
        value = ordered(mine, value, dp_swap(value, bit), axis)
    return value


def sum_group(partial_value, row, axis_size):
    kept = pick(partial_value, row, 2, 1)
    sent = pick(partial_value, 1 - row, 2, 1).astype(BF)
    half = (kept + swap(sent, "row").astype(F32)).astype(BF)
    return (half.astype(F32) + swap(half, "col").astype(F32)).astype(BF)


def shards(hidden_in, doc_lens, norm1_gain, wqkv, wout, norm2_gain, wi, wo, out_grad):
    tokens, _, width = hidden_in.shape
    half = 2 * width
    heads = width // HD
    hid = wo.shape[1]
    row, col = lax.axis_index("row"), lax.axis_index("col")
    index = lax.axis_index("dp")
    side = index % 2
    low_first = bits_of(lax.axis_size("dp"))
    high_first = low_first[1:] + low_first[:1]

    segment, position, occupied = layout(doc_lens[0], tokens)
    cosine_table, sine_table = rotary(position, HD)

    own = hidden_in[:, 0, :]
    hidden_half = ordered(col, own, swap(own, "col"), 1)
    hidden_other = swap(hidden_half, "row")
    residual = ordered(row, hidden_half, hidden_other, 1).astype(F32)
    gains = jnp.concatenate([norm1_gain, norm2_gain], axis=0)
    gains = ordered(col, gains, swap(gains, "col"), 1)
    gains = ordered(row, gains, swap(gains, "row"), 1)
    gain_one, gain_two = gains[0:1], gains[1:2]

    w_qkv = wqkv.reshape(half, 3, half)
    qkv_own = pick(w_qkv, col, 2, 2).reshape(half, 3 * width)
    qkv_got = swap(pick(w_qkv, 1 - col, 2, 2), "col").reshape(half, 3 * width)
    w_in = wi.reshape(2, width, 2, 2 * hid)
    in_first, in_last = w_in[..., :hid], w_in[..., hid:]
    in_own = jnp.where(col == 0, in_first, in_last).reshape(half, 2 * hid)
    in_send = jnp.where(
        col == 0,
        lax.dynamic_index_in_dim(in_last, side, 0, False),
        lax.dynamic_index_in_dim(in_first, side, 0, False),
    ).reshape(width, 2 * hid)
    in_got = swap(in_send, "col")
    in_got = ordered(side, in_got, dp_swap(in_got, 1), 0)

    grad_own = out_grad[:, 0, :]
    grad_half = ordered(col, grad_own, swap(grad_own, "col"), 1)
    mask = occupied.astype(BF)[:, None]
    down_half = grad_half * mask
    down_other = swap(down_half, "row")
    grad_top = ordered(row, down_half, down_other, 1).astype(F32)

    wo_rows = lax.dynamic_index_in_dim(wo, row, 0, False)[:, 0, :]
    wo_got = swap(lax.dynamic_index_in_dim(wo, 1 - row, 0, False)[:, 0, :], "row")
    out_rows = lax.dynamic_index_in_dim(wout, row, 0, False)[:, 0, :]
    out_got = swap(lax.dynamic_index_in_dim(wout, 1 - row, 0, False)[:, 0, :], "row")

    def by_col(value):
        split = value.reshape(tokens, 2, 2, width)
        mine = lax.dynamic_index_in_dim(split, col, 2, False).reshape(tokens, half)
        other = lax.dynamic_index_in_dim(split, 1 - col, 2, False).reshape(tokens, half)
        return mine, other

    normal_one, scale_one = norm_forward(residual)
    normed_one = (normal_one * gain_one).astype(BF)
    one_mine, one_other = by_col(normed_one)
    projected = dot(one_mine, qkv_own, NN) + dot(one_other, qkv_got, NN)
    projected = projected.reshape(tokens, 3, heads, HD)
    queries = rotate(projected[:, 0], cosine_table, sine_table).astype(BF)
    keys_all = rotate(projected[:, 1], cosine_table, sine_table).astype(BF)
    values_all = projected[:, 2].astype(BF)
    attended, logsums = attend_forward(queries, keys_all, values_all, segment)
    attended = attended.astype(BF).reshape(tokens, width)
    attended_all = ordered(row, attended, swap(attended, "row"), 1)
    w_out = wout.reshape(half, half)
    branch = dot(attended_all, w_out, NN).astype(BF)
    branch = (branch.astype(F32) + swap(branch, "col").astype(F32)).astype(BF)
    branch = ordered(row, branch, swap(branch, "row"), 1)
    middle = residual + branch.astype(F32)

    normal_two, scale_two = norm_forward(middle)
    normed_two = (normal_two * gain_two).astype(BF)
    two_mine, two_other = by_col(normed_two)
    gate_up = dot(two_mine, in_own, NN) + dot(two_other, in_got, NN)
    activated, gelu_pull = jax.vjp(geglu, gate_up[:, :hid], gate_up[:, hid:])
    activated = activated.astype(BF)
    activated_all = ordered(row, activated, swap(activated, "row"), 1)

    grad_hidden = dot(pick(grad_top, row, 2, 1).astype(BF), wo_rows, NT) + dot(
        pick(grad_top, 1 - row, 2, 1).astype(BF), wo_got, NT
    )
    grad_gate, grad_upper = gelu_pull(grad_hidden)
    grad_mix = jnp.concatenate([grad_gate, grad_upper], axis=1).astype(BF)
    grad_wi = jnp.concatenate(
        [dot(two_mine, grad_mix, TN).astype(BF)[None], dot(two_other, grad_mix, TN).astype(BF)[None]]
    )
    grad_wi = dp_scatter(grad_wi, low_first, 1)
    grad_wi_got = swap(grad_wi[1], "col")
    grad_wi = jnp.stack([grad_wi[0], grad_wi_got])
    grad_wi = dp_gather(grad_wi, low_first, 1).astype(F32).reshape(2, half, 2, hid)
    grad_wi = ordered(col, grad_wi[0], grad_wi[1], 2).reshape(wi.shape)

    grad_wo = dot(activated_all, down_half, TN).astype(BF)
    grad_wo = dp_gather(dp_scatter(grad_wo, high_first, 0), high_first, 0)
    grad_wo = grad_wo.astype(F32).reshape(wo.shape)

    w_down = wo.reshape(2 * hid, half)
    downward = dot(activated_all, w_down, NN)
    down_sent = pick(downward, 1 - col, 2, 1).astype(BF)
    downward = pick(downward, col, 2, 1) + swap(down_sent, "col").astype(F32)
    middle_own = pick(middle, 2 * row + col, 4, 1)
    hidden_out = (middle_own + downward).astype(BF)[:, None, :]

    def back(mine, other):
        mine = mine.reshape(tokens, 2, 1, width)
        other = other.reshape(tokens, 2, 1, width)
        return ordered(col, mine, other, 2).reshape(tokens, 4 * width)

    grad_two = back(dot(grad_mix, in_own, NT), dot(grad_mix, in_got, NT))
    grad_two = sum_group(grad_two, row, half)
    grad_two = ordered(row, grad_two, swap(grad_two, "row"), 1).astype(F32)
    grad_back_two, grad_gain_two = norm_backward(grad_two, normal_two, scale_two, gain_two)
    grad_middle = grad_top + grad_back_two
    grad_branch = grad_middle.astype(BF)
    branch_own = pick(grad_branch, row, 2, 1)
    branch_other = pick(grad_branch, 1 - row, 2, 1)
    grad_wout = dot(attended_all, branch_own, TN).astype(BF)
    grad_wout = dp_gather(dp_scatter(grad_wout, high_first, 0), high_first, 0)
    grad_wout = grad_wout.astype(F32).reshape(wout.shape)
    grad_attended = (dot(branch_own, out_rows, NT) + dot(branch_other, out_got, NT)).astype(BF)
    grad_attended = grad_attended.reshape(tokens, heads, HD)
    grad_queries, grad_keys, grad_values = attend_backward(
        queries, keys_all, values_all, grad_attended, logsums, segment
    )
    grad_queries = rotate_back(grad_queries, cosine_table, sine_table)
    grad_keys = rotate_back(grad_keys, cosine_table, sine_table)
    grad_proj = jnp.stack([grad_queries, grad_keys, grad_values], axis=1)
    grad_proj = grad_proj.reshape(tokens, 3 * width).astype(BF)
    grad_wqkv = jnp.concatenate(
        [dot(one_mine, grad_proj, TN).astype(BF)[None], dot(one_other, grad_proj, TN).astype(BF)[None]]
    )
    grad_wqkv = dp_scatter(grad_wqkv, low_first, 1)
    grad_wqkv = jnp.stack([grad_wqkv[0], swap(grad_wqkv[1], "col")])
    grad_wqkv = dp_gather(grad_wqkv, low_first, 1).astype(F32).reshape(2, half, 3, width)
    grad_wqkv = ordered(col, grad_wqkv[0], grad_wqkv[1], 2).reshape(wqkv.shape)

    grad_one = back(dot(grad_proj, qkv_own, NT), dot(grad_proj, qkv_got, NT))
    grad_one = sum_group(grad_one, row, half)
    grad_one = ordered(row, grad_one, swap(grad_one, "row"), 1).astype(F32)
    grad_back_one, grad_gain_one = norm_backward(grad_one, normal_one, scale_one, gain_one)
    grad_in = pick(grad_middle + grad_back_one, 2 * row + col, 4, 1)[:, None, :]

    small = jnp.concatenate(
        [
            pick(grad_gain_one, 2 * row + col, 4, 0)[None],
            pick(grad_gain_two, 2 * row + col, 4, 0)[None],
        ]
    )
    for bit in low_first:
        small = small + dp_swap(small, bit)
    return (
        hidden_out,
        grad_in,
        small[0:1],
        grad_wqkv,
        grad_wout,
        small[1:2],
        grad_wi,
        grad_wo,
    )


def solution(mesh):
    return jax.shard_map(
        shards,
        mesh=mesh,
        in_specs=(
            P("dp", "row", "col"),
            P("dp", None),
            P("row", "col"),
            P(None, "col", None, "row", None),
            P(None, "col", "row", None),
            P("row", "col"),
            P(None, "col", None, "row", None),
            P(None, "col", "row", None),
            P("dp", "row", "col"),
        ),
        out_specs=(
            P("dp", "row", "col"),
            P("dp", "row", "col"),
            P("row", "col"),
            P(None, "col", None, "row", None),
            P(None, "col", "row", None),
            P("row", "col"),
            P(None, "col", None, "row", None),
            P(None, "col", "row", None),
        ),
        check_vma=False,
    )
```

```python
import math

import jax
import jax.numpy as jnp
from jax import lax
from jax.experimental import pallas as pl
from jax.experimental.pallas import tpu as pltpu
from jax.sharding import PartitionSpec as P

HD = 64
EPSILON = 1e-05
ROPE_BASE = 160000.0
F32 = jnp.float32
BF = jnp.bfloat16
NN = ((1,), (0,))
NT = ((1,), (1,))
TN = ((0,), (0,))


def dot(left, right, dims=NN):
    return lax.dot_general(left, right, (dims, ((), ())), preferred_element_type=F32)


def swap(value, axis):
    return lax.ppermute(value, axis, [(0, 1), (1, 0)])


def dp_swap(value, bit):
    size = lax.axis_size("dp")
    return lax.ppermute(value, "dp", [(i, i ^ bit) for i in range(size)])


def ordered(index, mine, other, axis):
    return jnp.where(
        index == 0,
        jnp.concatenate([mine, other], axis),
        jnp.concatenate([other, mine], axis),
    )


def pick(value, index, parts, axis):
    size = value.shape[axis] // parts
    return lax.dynamic_slice_in_dim(value, index * size, size, axis)


def bits_of(size):
    assert size & (size - 1) == 0
    return [1 << k for k in range(size.bit_length() - 1)]


def call(kernel, outs, ids, *args, scratch=(), flops=0):
    outs = tuple(jax.ShapeDtypeStruct(s, d) for s, d in outs)
    moved = sum(math.prod(a.shape) * a.dtype.itemsize for a in args + outs)
    vmem = pl.BlockSpec(memory_space=pltpu.VMEM)
    return pl.pallas_call(
        kernel,
        out_shape=outs,
        in_specs=[pl.BlockSpec(memory_space=pltpu.SMEM)] + [vmem] * len(args),
        out_specs=tuple(vmem for _ in outs),
        scratch_shapes=list(scratch),
        compiler_params=pltpu.CompilerParams(vmem_limit_bytes=48 * 2**20),
        cost_estimate=pl.CostEstimate(flops=flops, bytes_accessed=moved, transcendentals=0),
    )(ids, *args)


def lanes(start, size):
    return pl.ds(pl.multiple_of(start, size), size)


def block(a, b, width):
    return lanes((2 * a + b) * width, width)


def normalize(values):
    centred = values - jnp.mean(values, axis=1, keepdims=True)
    scale = lax.rsqrt(jnp.mean(centred * centred, axis=1, keepdims=True) + EPSILON)
    return (centred * scale, scale)


def norm_backward(grad, normal, scale, gain):
    hat = grad * gain
    correction = (
        hat
        - jnp.mean(hat, axis=1, keepdims=True)
        - normal * jnp.mean(hat * normal, axis=1, keepdims=True)
    )
    return scale * correction


def row_steps(count):
    step = 128 if count % 128 == 0 else count
    return [pl.ds(i, step) for i in range(0, count, step)]


def norm_kernel(ids, own, own_x, others, gain, hidden, normed):
    r, c = ids[0], ids[1]
    width = own.shape[1]
    hidden[:, block(r, c, width)] = own[...]
    hidden[:, block(r, 1 - c, width)] = own_x[...]
    hidden[:, block(1 - r, c, width)] = others[0]
    hidden[:, block(1 - r, 1 - c, width)] = others[1]
    for rows in row_steps(own.shape[0]):
        normal, _ = normalize(hidden[rows, :].astype(F32))
        normed[rows, :] = (normal * gain[...]).astype(BF)


def turn(values, lane):
    size = values.shape[1]
    half = HD // 2
    return jnp.where(
        lane % HD < half, -pltpu.roll(values, size - half, 1), pltpu.roll(values, half, 1)
    )


def segments(ids, shape, axis):
    places = lax.broadcasted_iota(jnp.int32, shape, axis)
    total = jnp.zeros(shape, jnp.int32)
    for j in range(4, ids.shape[0]):
        total = total + (places >= ids[j]).astype(jnp.int32)
    return total


def attend_kernel(ids, normed, w_own, w_got, cosine, sine, qkv, attended, probs):
    c = ids[1]
    tokens = normed.shape[0]
    width = w_got.shape[3]
    lane = lax.broadcasted_iota(jnp.int32, (tokens, width), 1)
    for s in range(3):
        total = None
        for a in range(2):
            part = dot(normed[:, block(a, c, width)], w_own[a, s, :, lanes(c * width, width)])
            part += dot(normed[:, block(a, 1 - c, width)], w_got[a, s])
            total = part if total is None else total + part
        if s < 2:
            total = total * cosine[...] + turn(total, lane) * sine[...]
        qkv[:, s * width : (s + 1) * width] = total.astype(BF)
    pair = 2 * HD
    factor = HD**-0.5
    keys_segment = segments(ids, (1, tokens), 1)
    step = min(256, tokens)
    for start in range(0, tokens, step):
        rows = slice(start, start + step)
        same = (segments(ids, (tokens, 1), 0)[rows]) == keys_segment
        low = lax.broadcasted_iota(jnp.int32, (step, pair), 1) < HD
        for h in range(0, width, pair):
            query = qkv[rows, h : h + pair]
            key = qkv[:, width + h : width + h + pair]
            value = qkv[:, 2 * width + h : 2 * width + h + pair]
            results = []
            for side in range(2):
                mine = low if side == 0 else jnp.logical_not(low)
                scores = dot(jnp.where(mine, query, jnp.zeros_like(query)), key, NT) * factor
                scores = jnp.where(same, scores, -1e30)
                raised = jnp.exp(scores - jnp.max(scores, axis=1, keepdims=True))
                weights = (raised / jnp.sum(raised, axis=1, keepdims=True)).astype(BF)
                probs[h // HD + side, rows, :] = weights
                results.append(dot(weights, value))
            attended[rows, h : h + pair] = jnp.where(low, results[0], results[1]).astype(BF)


def attend_back_kernel(ids, qkv, probs, grad, cosine, sine, out):
    tokens = qkv.shape[0]
    width = qkv.shape[1] // 3
    pair = 2 * HD
    factor = HD**-0.5
    low = lax.broadcasted_iota(jnp.int32, (tokens, pair), 1) < HD
    lane = lax.broadcasted_iota(jnp.int32, (tokens, pair), 1)
    for h in range(0, width, pair):
        query = qkv[:, h : h + pair]
        key = qkv[:, width + h : width + h + pair]
        value = qkv[:, 2 * width + h : 2 * width + h + pair]
        top = grad[:, h : h + pair]
        parts = []
        for side in range(2):
            mine = low if side == 0 else jnp.logical_not(low)
            weights = probs[h // HD + side]
            grad_values = dot(weights, top, TN)
            grad_probs = dot(jnp.where(mine, top, jnp.zeros_like(top)), value, NT)
            wide = weights.astype(F32)
            product = wide * grad_probs
            grad_scores = (product - wide * jnp.sum(product, axis=1, keepdims=True)).astype(BF)
            parts.append(
                (
                    dot(grad_scores, key) * factor,
                    dot(grad_scores, query, TN) * factor,
                    grad_values,
                )
            )
        for s in range(3):
            total = jnp.where(low, parts[0][s], parts[1][s])
            if s < 2:
                total = total * cosine[:, :pair] - turn(total, lane) * sine[:, :pair]
            out[:, s * width + h : s * width + h + pair] = total.astype(BF)


def branch_kernel(ids, own, other, wout, out):
    r = ids[0]
    out[...] = (dot(own[...], wout[r]) + dot(other[...], wout[1 - r])).astype(BF)


def ffn_kernel(
    ids, hidden, br_own, br_got, gain, wi, got_y, got_n, gd_own, gd_got, wo, wo_got,
    middle, normed, activated, mix,
):
    r, c, y = ids[0], ids[1], ids[2]
    half = br_own.shape[1]
    width = half // 2
    hid = activated.shape[1]
    here, there = lanes(r * half, half), lanes((1 - r) * half, half)
    middle[:, here] = hidden[:, here].astype(F32) + br_own[...].astype(F32)
    middle[:, there] = hidden[:, there].astype(F32) + br_got[...].astype(F32)
    for rows in row_steps(hidden.shape[0]):
        normal, _ = normalize(middle[rows, :])
        normed[rows, :] = (normal * gain[...]).astype(BF)
    cols = pl.ds(pl.multiple_of(c * hid, 16), hid)
    step = 256
    for start in range(0, hidden.shape[0], step):
        rows = pl.ds(start, step)
        parts = []
        for g in range(2):
            total = dot(normed[rows, block(0, c, width)], wi[0, g, cols, :], NT)
            total += dot(normed[rows, block(1, c, width)], wi[1, g, cols, :], NT)
            total += dot(normed[rows, block(y, 1 - c, width)], got_y[g], NT)
            total += dot(normed[rows, block(1 - y, 1 - c, width)], got_n[g], NT)
            parts.append(total)
        gate, up = parts
        grad = dot(gd_own[rows, :], wo[r], NT) + dot(gd_got[rows, :], wo_got[...], NT)
        cdf = 0.5 + 0.5 * lax.erf(gate * (0.5**0.5))
        pdf = jnp.exp(-0.5 * gate * gate) * ((2.0 * math.pi) ** -0.5)
        gelu = gate * cdf
        activated[rows, :] = (gelu * up).astype(BF)
        mix[0, rows, :] = (grad * up * (cdf + gate * pdf)).astype(BF)
        mix[1, rows, :] = (grad * gelu).astype(BF)


def pieces(count, parts):
    size = -(-count // (16 * parts)) * 16
    return size, [min(j * size, count - size) for j in range(parts)]


def wi_kernel(ids, mix, normed, out):
    c = ids[1]
    width = normed.shape[1] // 4
    size, starts = pieces(mix.shape[2], out.shape[2])
    right = jnp.concatenate(
        [normed[:, block(a, b, width)] for a in range(2) for b in (c, 1 - c)], axis=1
    )
    for g in range(2):
        total = dot(mix[g], right, TN).astype(BF)
        for k in range(4):
            for j, start in enumerate(starts):
                out[k // 2, g, j, k % 2] = total[start : start + size, k * width : (k + 1) * width]


def wo_kernel(ids, own, other, down, out):
    r = ids[0]
    width = down.shape[1] // 2
    size, starts = pieces(own.shape[1], out.shape[2])
    for a, ref in ((r, own), (1 - r, other)):
        total = dot(ref[...], down[...], TN).astype(BF)
        for l in range(2):
            for j, start in enumerate(starts):
                out[a, l, j] = total[start : start + size, l * width : (l + 1) * width]


def down_kernel(ids, own, other, wo, middle, kept, sent):
    r, c = ids[0], ids[1]
    width = kept.shape[1]
    for b, ref in ((c, kept), (1 - c, sent)):
        cols = lanes(b * width, width)
        total = dot(own[...], wo[r, :, cols]) + dot(other[...], wo[1 - r, :, cols])
        if ref is kept:
            total = total + middle[:, block(r, c, width)]
        ref[...] = total.astype(ref.dtype)


def split_sum(ids, work, kept, sent):
    r = ids[0]
    kept[...] = work[r]
    sent[...] = work[1 - r].astype(BF)


def ffn_back_kernel(ids, mix, wi, got_y, got_n, kept, sent, work):
    c, y = ids[1], ids[2]
    width = kept.shape[1] // 2
    hid = mix.shape[2]
    cols = pl.ds(pl.multiple_of(c * hid, 16), hid)
    for a in range(2):
        work[a, :, lanes(c * width, width)] = dot(mix[0], wi[a, 0, cols, :]) + dot(
            mix[1], wi[a, 1, cols, :]
        )
    for a, got in ((y, got_y), (1 - y, got_n)):
        work[a, :, lanes((1 - c) * width, width)] = dot(mix[0], got[0]) + dot(mix[1], got[1])
    split_sum(ids, work, kept, sent)


def qkv_back_kernel(ids, grad, w_own, w_got, kept, sent, work):
    c = ids[1]
    width = kept.shape[1] // 2
    for a in range(2):
        for b in range(2):
            total = None
            for s in range(3):
                left = grad[:, s * width : (s + 1) * width]
                right = w_own[a, s, :, lanes(c * width, width)] if b == 0 else w_got[a, s]
                part = dot(left, right, NT)
                total = part if total is None else total + part
            where = c if b == 0 else 1 - c
            work[a, :, lanes(where * width, width)] = total
    split_sum(ids, work, kept, sent)


def middle_back_kernel(
    ids, g_own, g_got, middle, gain, gd_own, gd_got, wout, wout_got,
    grad_middle, branch_own, attended, gain_grad, work,
):
    r = ids[0]
    half = g_own.shape[1]
    here, there = lanes(r * half, half), lanes((1 - r) * half, half)
    work[:, here] = g_own[...].astype(F32)
    work[:, there] = g_got[...].astype(F32)
    grad_middle[:, here] = gd_own[...].astype(F32)
    grad_middle[:, there] = gd_got[...].astype(F32)
    total = None
    for rows in row_steps(g_own.shape[0]):
        normal, scale = normalize(middle[rows, :])
        grad = work[rows, :]
        grad_middle[rows, :] += norm_backward(grad, normal, scale, gain[...])
        part = jnp.sum(grad * normal, axis=0, keepdims=True)
        total = part if total is None else total + part
    gain_grad[...] = total
    branch_own[...] = grad_middle[:, here].astype(BF)
    other = grad_middle[:, there].astype(BF)
    attended[...] = (
        dot(branch_own[...], wout[r], NT) + dot(other, wout_got[...], NT)
    ).astype(BF)


def input_back_kernel(
    ids, g_own, g_got, hidden, gain, grad_middle, grad_in, gain_grad, work
):
    r, c = ids[0], ids[1]
    half = g_own.shape[1]
    work[:, lanes(r * half, half)] = g_own[...].astype(F32)
    work[:, lanes((1 - r) * half, half)] = g_got[...].astype(F32)
    total = None
    for rows in row_steps(g_own.shape[0]):
        normal, scale = normalize(hidden[rows, :].astype(F32))
        grad = work[rows, :]
        work[rows, :] = grad_middle[rows, :] + norm_backward(grad, normal, scale, gain[...])
        part = jnp.sum(grad * normal, axis=0, keepdims=True)
        total = part if total is None else total + part
    gain_grad[...] = total
    grad_in[...] = work[:, block(r, c, half // 2)]


def last_kernel(ids, normed, proj, att_own, att_got, branch, out):
    r, c = ids[0], ids[1]
    count, rows = out.shape[0], out.shape[1]
    width = att_own.shape[1]
    side = 3 * width
    per = count // 2
    for a in range(2):
        for b in range(2):
            where = c if b == 0 else 1 - c
            total = dot(normed[:, block(a, where, width)], proj[...], TN).astype(BF)
            for j in range(per):
                out[a * per + j, :, b * side : (b + 1) * side] = total[j * rows : (j + 1) * rows]
    for a, ref in ((r, att_own), (1 - r, att_got)):
        total = dot(ref[...], branch[...], TN).astype(BF)
        for j in range(per):
            out[a * per + j, :, 2 * side :] = total[j * rows : (j + 1) * rows]


def merged(ids, first, second):
    count = first.shape[0]
    for ref, flip in ((first, 0), (second, count)):
        for m in range(count):
            yield ids[3] ^ (m + flip), ref, m


def wi_out_kernel(ids, first, second, out):
    c = ids[1]
    size = first.shape[2]
    hid = out.shape[2] // 2
    parts = first.shape[0] // 2
    for place, ref, m in merged(ids, first, second):
        a, g, j = place // (2 * parts), (place // parts) % 2, place % parts
        start = jnp.minimum(j * size, hid - size)
        for b in range(2):
            where = c if b == 0 else 1 - c
            rows = pl.ds(pl.multiple_of(where * hid + start, 16), size)
            out[a, g, rows, :] = ref[m, b].astype(F32)


def wo_out_kernel(ids, first, second, out):
    size, width = first.shape[1], first.shape[2]
    hid = out.shape[1]
    parts = first.shape[0] // 2
    for place, ref, m in merged(ids, first, second):
        a, l, j = place // (2 * parts), (place // parts) % 2, place % parts
        rows = pl.ds(pl.multiple_of(jnp.minimum(j * size, hid - size), 16), size)
        out[a, rows, lanes(l * width, width)] = ref[m]


def last_out_kernel(ids, first, second, qkv, wout):
    c = ids[1]
    size = first.shape[1]
    half = wout.shape[1]
    width = half // 2
    for place, ref, m in merged(ids, first, second):
        rows = pl.ds(pl.multiple_of(place * size, size), size)
        for b in range(2):
            where = c if b == 0 else 1 - c
            for s in range(3):
                start = (3 * b + s) * width
                qkv[rows, lanes(s * half + where * width, width)] = ref[
                    m, :, start : start + width
                ]
        wout[rows, :] = ref[m, :, 6 * width :]


def dp_scatter(value, order):
    index = lax.axis_index("dp")
    parts = [value]
    for bit in order:
        mine = (index // bit) % 2

        def side(which):
            total = None
            for part in parts:
                piece = pick(part, which, 2, 0).astype(F32)
                total = piece if total is None else total + piece
            return total.astype(BF)

        sent, kept = side(1 - mine), side(mine)
        parts = [kept, dp_swap(sent, bit)]
    return (parts[0].astype(F32) + parts[1].astype(F32)).astype(BF)


def dp_gather(value, order):
    for bit in order[:0:-1]:
        value = jnp.concatenate([value, dp_swap(value, bit)], axis=0)
    return value, dp_swap(value, order[0])


def place_of(order):
    index = lax.axis_index("dp")
    place = jnp.int32(0)
    for bit in order:
        place = 2 * place + (index // bit) % 2
    return place.astype(jnp.int32)


def sum_group(kept, sent):
    half = (kept + swap(sent, "row").astype(F32)).astype(BF)
    half = (half.astype(F32) + swap(half, "col").astype(F32)).astype(BF)
    return half, swap(half, "row")


def shards(hidden_in, doc_lens, norm1_gain, wqkv, wout, norm2_gain, wi, wo, out_grad):
    tokens, _, width = hidden_in.shape
    half, full = 2 * width, 4 * width
    hid = wo.shape[1]
    count = lax.axis_size("dp")
    row, col = lax.axis_index("row"), lax.axis_index("col")
    side = lax.axis_index("dp") % 2
    low_first = bits_of(count)
    high_first = low_first[1:] + low_first[:1]
    ends = jnp.cumsum(doc_lens[0])
    head = [row, col, side]
    ids = jnp.concatenate([jnp.stack(head + [place_of(low_first)]).astype(jnp.int32), ends])
    ids_high = jnp.concatenate([jnp.stack(head + [place_of(high_first)]).astype(jnp.int32), ends])

    places = jnp.arange(tokens, dtype=jnp.int32)
    passed = ends[None, :] <= places[:, None]
    doc_start = jnp.sum(jnp.where(passed, doc_lens[0][None, :], 0), axis=1)
    occupied = (places < ends[-1]).astype(BF)[:, None]
    frequency = jnp.exp(
        jnp.arange(HD // 2, dtype=F32) * (-2.0 * math.log(ROPE_BASE) / HD)
    )
    angles = (places - doc_start).astype(F32)[:, None] * frequency[None, :]
    tables = lax.optimization_barrier((jnp.cos(angles), jnp.sin(angles)))
    cosine, sine = [jnp.tile(t, (1, 2 * width // HD)) for t in tables]

    own = hidden_in[:, 0, :]
    own_x = swap(own, "col")
    others = swap(jnp.stack([own, own_x]), "row")
    gains = jnp.concatenate([norm1_gain, norm2_gain], axis=0)
    gains = ordered(col, gains, swap(gains, "col"), 1)
    gains = ordered(row, gains, swap(gains, "row"), 1)
    gain_one, gain_two = gains[0:1], gains[1:2]

    w_qkv = wqkv.transpose(0, 2, 3, 1, 4).reshape(2, 3, width, half)
    qkv_got = swap(pick(w_qkv, 1 - col, 2, 3), "col")
    w_in = wi.transpose(0, 2, 3, 4, 1).reshape(2, 2, 2 * hid, width)
    in_send = lax.dynamic_slice(
        w_in, (side, 0, (1 - col) * hid, 0), (1, 2, hid, width)
    )[0]
    in_y = swap(in_send, "col")
    in_n = dp_swap(in_y, 1)
    w_down = wo.reshape(2, hid, half)
    down_got = swap(lax.dynamic_index_in_dim(w_down, 1 - row, 0, False), "row")
    w_out = wout.reshape(2, width, half)
    out_got = swap(lax.dynamic_index_in_dim(w_out, 1 - row, 0, False), "row")

    grad_own = out_grad[:, 0, :] * occupied
    grad_half = ordered(col, grad_own, swap(grad_own, "col"), 1)
    grad_other = swap(grad_half, "row")

    hidden, normed_one = call(
        norm_kernel,
        (((tokens, full), BF), ((tokens, full), BF)),
        ids, own, own_x, others, gain_one,
    )
    qkv, attended, probs = call(
        attend_kernel,
        (((tokens, 3 * width), BF), ((tokens, width), BF), ((width // HD, tokens, tokens), BF)),
        ids, normed_one, w_qkv, qkv_got, cosine, sine,
        flops=2 * tokens * full * 3 * width,
    )
    attended_got = swap(attended, "row")
    (branch,) = call(
        branch_kernel, (((tokens, half), BF),), ids, attended, attended_got, w_out,
        flops=2 * tokens * half * half,
    )
    branch = (branch.astype(F32) + swap(branch, "col").astype(F32)).astype(BF)
    branch_got = swap(branch, "row")

    middle, normed_two, activated, mix = call(
        ffn_kernel,
        (
            ((tokens, full), F32), ((tokens, full), BF), ((tokens, hid), BF),
            ((2, tokens, hid), BF),
        ),
        ids, hidden, branch, branch_got, gain_two, w_in, in_y, in_n, grad_half, grad_other,
        w_down, down_got,
        flops=6 * tokens * full * hid,
    )
    parts = max(count // 4, 1)
    size, _ = pieces(hid, parts)
    (grad_wi,) = call(
        wi_kernel, (((2, 2, parts, 2, size, width), BF),), ids, mix, normed_two,
        flops=4 * tokens * full * hid,
    )
    grad_wi = dp_scatter(grad_wi.reshape(count, 2, size, width), low_first)
    activated_got = swap(activated, "row")
    (grad_wo,) = call(
        wo_kernel, (((2, 2, parts, size, width), BF),), ids, activated, activated_got, grad_half,
        flops=4 * tokens * half * hid,
    )
    grad_wo = dp_scatter(grad_wo.reshape(count, size, width), high_first)
    kept, sent = call(
        ffn_back_kernel,
        (((tokens, half), F32), ((tokens, half), BF)),
        ids, mix, w_in, in_y, in_n,
        scratch=[pltpu.VMEM((2, tokens, half), F32)],
        flops=4 * tokens * full * hid,
    )
    two_own, two_got = sum_group(kept, sent)
    grad_middle, branch_grad, grad_attended, gain_two_grad = call(
        middle_back_kernel,
        (
            ((tokens, full), F32), ((tokens, half), BF), ((tokens, width), BF), ((1, full), F32),
        ),
        ids, two_own, two_got, middle, gain_two, grad_half, grad_other, w_out, out_got,
        scratch=[pltpu.VMEM((tokens, full), F32)],
        flops=2 * tokens * full * width,
    )
    (grad_proj,) = call(
        attend_back_kernel,
        (((tokens, 3 * width), BF),),
        ids, qkv, probs, grad_attended, cosine, sine,
        flops=8 * tokens * tokens * 2 * width,
    )
    rows = half // count
    (grad_last,) = call(
        last_kernel,
        (((count, rows, 8 * width), BF),),
        ids, normed_one, grad_proj, attended, attended_got, branch_grad,
        flops=2 * tokens * full * 4 * width,
    )
    grad_last = dp_scatter(grad_last, low_first)
    kept, sent = call(
        qkv_back_kernel,
        (((tokens, half), F32), ((tokens, half), BF)),
        ids, grad_proj, w_qkv, qkv_got,
        scratch=[pltpu.VMEM((2, tokens, half), F32)],
        flops=2 * tokens * full * 3 * width,
    )
    one_own, one_got = sum_group(kept, sent)
    grad_in, gain_one_grad = call(
        input_back_kernel,
        (((tokens, width), F32), ((1, full), F32)),
        ids, one_own, one_got, hidden, gain_one, grad_middle,
        scratch=[pltpu.VMEM((tokens, full), F32)],
    )

    kept, sent = call(
        down_kernel,
        (((tokens, width), F32), ((tokens, width), BF)),
        ids, activated, activated_got, w_down, middle,
        flops=4 * tokens * half * hid,
    )
    hidden_out = (kept + swap(sent, "col").astype(F32)).astype(BF)

    grad_wi = jnp.concatenate([grad_wi[:, :1], swap(grad_wi[:, 1:], "col")], axis=1)
    first, second = dp_gather(grad_wi, low_first)
    (grad_wi,) = call(
        wi_out_kernel, (((2, 2, 2 * hid, width), F32),), ids, first, second
    )
    grad_wi = grad_wi.reshape(2, 2, 1, 2 * hid, width).transpose(0, 4, 1, 2, 3)
    first, second = dp_gather(grad_wo, high_first)
    (grad_wo,) = call(wo_out_kernel, (((2, hid, half), BF),), ids_high, first, second)
    side_lanes = 3 * width
    grad_last = jnp.concatenate(
        [
            grad_last[..., :side_lanes],
            swap(grad_last[..., side_lanes : 2 * side_lanes], "col"),
            grad_last[..., 2 * side_lanes :],
        ],
        axis=2,
    )
    first, second = dp_gather(grad_last, low_first)
    grad_wqkv, grad_wout = call(
        last_out_kernel,
        (((half, 3 * half), BF), ((half, half), BF)),
        ids, first, second,
    )
    mine = 2 * row + col
    small = jnp.concatenate([pick(gain_one_grad, mine, 4, 1), pick(gain_two_grad, mine, 4, 1)])
    for bit in low_first:
        small = small + dp_swap(small, bit)
    return (
        hidden_out[:, None, :],
        grad_in[:, None, :],
        small[0:1],
        grad_wqkv.astype(F32).reshape(2, width, 3, 1, half),
        grad_wout.astype(F32).reshape(wout.shape),
        small[1:2],
        grad_wi,
        grad_wo.astype(F32).reshape(wo.shape),
    )


def solution(mesh):
    return jax.shard_map(
        shards,
        mesh=mesh,
        in_specs=(
            P("dp", "row", "col"),
            P("dp", None),
            P("row", "col"),
            P(None, "col", None, "row", None),
            P(None, "col", "row", None),
            P("row", "col"),
            P(None, "col", None, "row", None),
            P(None, "col", "row", None),
            P("dp", "row", "col"),
        ),
        out_specs=(
            P("dp", "row", "col"),
            P("dp", "row", "col"),
            P("row", "col"),
            P(None, "col", None, "row", None),
            P(None, "col", "row", None),
            P("row", "col"),
            P(None, "col", None, "row", None),
            P(None, "col", "row", None),
        ),
        check_vma=False,
    )
```

```python
import functools
import math

import jax
import jax.numpy as jnp
from jax import lax
from jax.experimental import pallas as pl
from jax.experimental.pallas import tpu as pltpu
from jax.sharding import PartitionSpec as P

HD = 64
EPSILON = 1e-05
ROPE_BASE = 160000.0
F32 = jnp.float32
BF = jnp.bfloat16
LATE = (
    "W2", "L2", "L1", "G", "W1", "W2", "L2", "L1", "O", "G", "W2", "L2", "W1", "L1", "O",
    "W2", "L2", "G",
)
NN = ((1,), (0,))
NT = ((1,), (1,))
TN = ((0,), (0,))


def dot(left, right, dims=NN):
    return lax.dot_general(left, right, (dims, ((), ())), preferred_element_type=F32)


def swap(value, axis):
    return lax.ppermute(value, axis, [(0, 1), (1, 0)])


def dp_swap(value, bit):
    size = lax.axis_size("dp")
    return lax.ppermute(value, "dp", [(i, i ^ bit) for i in range(size)])


def ordered(index, mine, other, axis):
    return jnp.where(
        index == 0,
        jnp.concatenate([mine, other], axis),
        jnp.concatenate([other, mine], axis),
    )


def pick(value, index, parts, axis):
    size = value.shape[axis] // parts
    return lax.dynamic_slice_in_dim(value, index * size, size, axis)


def bits_of(size):
    assert size & (size - 1) == 0
    return [1 << k for k in range(size.bit_length() - 1)]


def call(kernel, outs, ids, *args, scratch=()):
    outs = tuple(jax.ShapeDtypeStruct(s, d) for s, d in outs)
    vmem = pl.BlockSpec(memory_space=pltpu.VMEM)
    return pl.pallas_call(
        kernel,
        out_shape=outs,
        in_specs=[pl.BlockSpec(memory_space=pltpu.SMEM)] + [vmem] * len(args),
        out_specs=tuple(vmem for _ in outs),
        scratch_shapes=list(scratch),
        compiler_params=pltpu.CompilerParams(vmem_limit_bytes=36 * 2**20),
        cost_estimate=pl.CostEstimate(
            flops=1024, bytes_accessed=1024, transcendentals=0
        ),
    )(ids, *args)


def lanes(start, size):
    return pl.ds(pl.multiple_of(start, size), size)


def block(a, b, width):
    return lanes((2 * a + b) * width, width)


def normalize(values):
    centred = values - jnp.mean(values, axis=1, keepdims=True)
    scale = lax.rsqrt(jnp.mean(centred * centred, axis=1, keepdims=True) + EPSILON)
    return (centred * scale, scale)


def norm_backward(grad, normal, scale, gain):
    hat = grad * gain
    correction = (
        hat
        - jnp.mean(hat, axis=1, keepdims=True)
        - normal * jnp.mean(hat * normal, axis=1, keepdims=True)
    )
    return scale * correction


def row_steps(count):
    step = 128 if count % 128 == 0 else count
    return [pl.ds(i, step) for i in range(0, count, step)]


def norm_kernel(ids, own, own_x, others, gain, hidden, normed):
    r, c = ids[0], ids[1]
    width = own.shape[1]
    hidden[:, block(r, c, width)] = own[...]
    hidden[:, block(r, 1 - c, width)] = own_x[...]
    hidden[:, block(1 - r, c, width)] = others[0]
    hidden[:, block(1 - r, 1 - c, width)] = others[1]
    for rows in row_steps(own.shape[0]):
        normal, _ = normalize(hidden[rows, :].astype(F32))
        normed[rows, :] = (normal * gain[...]).astype(BF)


def turn(values, lane):
    size = values.shape[1]
    half = HD // 2
    return jnp.where(
        lane % HD < half, -pltpu.roll(values, size - half, 1), pltpu.roll(values, half, 1)
    )


def segments(ids, shape, axis):
    places = lax.broadcasted_iota(jnp.int32, shape, axis)
    total = jnp.zeros(shape, jnp.int32)
    for j in range(6, ids.shape[0]):
        total = total + (places >= ids[j]).astype(jnp.int32)
    return total


def attend_kernel(ids, normed, w_own, got_y, got_n, cosine, sine, qkv, attended, probs):
    c, y = ids[1], ids[2]
    tokens = normed.shape[0]
    width = got_y.shape[2]
    lane = lax.broadcasted_iota(jnp.int32, (tokens, width), 1)
    for s in range(3):
        total = None
        for a, got in ((y, got_y), (1 - y, got_n)):
            part = dot(normed[:, block(a, c, width)], w_own[a, s, :, lanes(c * width, width)])
            part += dot(normed[:, block(a, 1 - c, width)], got[s])
            total = part if total is None else total + part
        if s < 2:
            total = total * cosine[...] + turn(total, lane) * sine[...]
        qkv[:, s * width : (s + 1) * width] = total.astype(BF)
    pair = 2 * HD
    factor = HD**-0.5
    keys_segment = segments(ids, (1, tokens), 1)
    step = min(256, tokens)
    for start in range(0, tokens, step):
        rows = slice(start, start + step)
        same = (segments(ids, (tokens, 1), 0)[rows]) == keys_segment
        low = lax.broadcasted_iota(jnp.int32, (step, pair), 1) < HD
        for h in range(0, width, pair):
            query = qkv[rows, h : h + pair]
            key = qkv[:, width + h : width + h + pair]
            value = qkv[:, 2 * width + h : 2 * width + h + pair]
            results = []
            for side in range(2):
                mine = low if side == 0 else jnp.logical_not(low)
                scores = dot(jnp.where(mine, query, jnp.zeros_like(query)), key, NT) * factor
                scores = jnp.where(same, scores, -1e30)
                raised = jnp.exp(scores - jnp.max(scores, axis=1, keepdims=True))
                weights = (raised / jnp.sum(raised, axis=1, keepdims=True)).astype(BF)
                probs[h // HD + side, rows, :] = weights
                results.append(dot(weights, value))
            attended[rows, h : h + pair] = jnp.where(low, results[0], results[1]).astype(BF)


def attend_back_kernel(ids, qkv, probs, grad, cosine, sine, out):
    tokens = qkv.shape[0]
    width = qkv.shape[1] // 3
    pair = 2 * HD
    factor = HD**-0.5
    low = lax.broadcasted_iota(jnp.int32, (tokens, pair), 1) < HD
    lane = lax.broadcasted_iota(jnp.int32, (tokens, pair), 1)
    for h in range(0, width, pair):
        query = qkv[:, h : h + pair]
        key = qkv[:, width + h : width + h + pair]
        value = qkv[:, 2 * width + h : 2 * width + h + pair]
        top = grad[:, h : h + pair]
        parts = []
        for side in range(2):
            mine = low if side == 0 else jnp.logical_not(low)
            weights = probs[h // HD + side]
            grad_values = dot(weights, top, TN)
            grad_probs = dot(jnp.where(mine, top, jnp.zeros_like(top)), value, NT)
            wide = weights.astype(F32)
            product = wide * grad_probs
            grad_scores = (product - wide * jnp.sum(product, axis=1, keepdims=True)).astype(BF)
            parts.append(
                (
                    dot(grad_scores, key) * factor,
                    dot(grad_scores, query, TN) * factor,
                    grad_values,
                )
            )
        for s in range(3):
            total = jnp.where(low, parts[0][s], parts[1][s])
            if s < 2:
                total = total * cosine[:, :pair] - turn(total, lane) * sine[:, :pair]
            out[:, s * width + h : s * width + h + pair] = total.astype(BF)


def branch_kernel(ids, own, other, wout, out):
    r = ids[0]
    out[...] = (dot(own[...], wout[r]) + dot(other[...], wout[1 - r])).astype(BF)


def ffn_kernel(
    ids, hidden, br_own, br_got, gain, wi, got_y, got_n, gd_own, gd_got, wo, wo_got,
    middle, normed, activated, mix,
):
    r, c, y = ids[0], ids[1], ids[2]
    half = br_own.shape[1]
    width = half // 2
    hid = mix.shape[2]
    here, there = lanes(r * half, half), lanes((1 - r) * half, half)
    middle[:, here] = hidden[:, here].astype(F32) + br_own[...].astype(F32)
    middle[:, there] = hidden[:, there].astype(F32) + br_got[...].astype(F32)
    for rows in row_steps(hidden.shape[0]):
        normal, _ = normalize(middle[rows, :])
        normed[rows, :] = (normal * gain[...]).astype(BF)
    cols = pl.ds(pl.multiple_of(c * hid, 16), hid)
    step = 256
    for start in range(0, hidden.shape[0], step):
        rows = pl.ds(start, step)
        parts = []
        for g in range(2):
            total = dot(normed[rows, block(0, c, width)], wi[0, g, cols, :], NT)
            total += dot(normed[rows, block(1, c, width)], wi[1, g, cols, :], NT)
            total += dot(normed[rows, block(y, 1 - c, width)], got_y[g], NT)
            total += dot(normed[rows, block(1 - y, 1 - c, width)], got_n[g], NT)
            parts.append(total)
        gate, up = parts
        grad = dot(gd_own[rows, :], wo[r], NT) + dot(gd_got[rows, :], wo_got[...], NT)
        cdf = 0.5 + 0.5 * lax.erf(gate * (0.5**0.5))
        pdf = jnp.exp(-0.5 * gate * gate) * ((2.0 * math.pi) ** -0.5)
        gelu = gate * cdf
        activated[rows, :hid] = (gelu * up).astype(BF)
        mix[0, rows, :] = (grad * up * (cdf + gate * pdf)).astype(BF)
        mix[1, rows, :] = (grad * gelu).astype(BF)


def pieces(count, parts):
    size = -(-count // (16 * parts)) * 16
    return size, [min(j * size, count - size) for j in range(parts)]


def wi_kernel(ids, mix, normed, kept_own, sent_own, kept_far, sent_far):
    c, y, z = ids[1], ids[2], ids[4]
    width = normed.shape[1] // 4
    size, starts = pieces(mix.shape[2], kept_own.shape[1])
    outs = (kept_own, sent_own, kept_far, sent_far)
    places = ((y, c), (1 - y, c), (z, 1 - c), (1 - z, 1 - c))
    right = jnp.concatenate([normed[:, block(a, b, width)] for a, b in places], axis=1)
    for g in range(2):
        total = dot(mix[g], right, TN).astype(BF)
        for k, out in enumerate(outs):
            for j, start in enumerate(starts):
                out[g, j] = total[start : start + size, k * width : (k + 1) * width]


def wo_kernel(hid, ids, own, other, down, kept, sent):
    r, y = ids[0], ids[4]
    width = down.shape[1] // 2
    size, starts = pieces(hid, kept.shape[1])
    right = jnp.concatenate([down[:, lanes(l * width, width)] for l in (y, 1 - y)], axis=1)
    for a, ref in ((r, own), (1 - r, other)):
        total = dot(ref[:, :hid], right, TN).astype(BF)
        for k, out in enumerate((kept, sent)):
            for j, start in enumerate(starts):
                out[a, j] = total[start : start + size, k * width : (k + 1) * width]


def down_kernel(ids, own, other, wo, middle, kept, sent):
    r, c = ids[0], ids[1]
    width = kept.shape[1]
    hid = wo.shape[1]
    for b, ref in ((c, kept), (1 - c, sent)):
        cols = lanes(b * width, width)
        total = dot(own[:, :hid], wo[r, :, cols]) + dot(other[:, :hid], wo[1 - r, :, cols])
        if ref is kept:
            total = total + middle[:, block(r, c, width)]
        ref[...] = total.astype(ref.dtype)


def split_sum(ids, work, kept, sent):
    r = ids[0]
    kept[...] = work[r]
    sent[...] = work[1 - r].astype(BF)


def ffn_back_kernel(ids, mix, wi, got_y, got_n, kept, sent, work):
    c, y = ids[1], ids[2]
    width = kept.shape[1] // 2
    hid = mix.shape[2]
    cols = pl.ds(pl.multiple_of(c * hid, 16), hid)
    for a in range(2):
        work[a, :, lanes(c * width, width)] = dot(mix[0], wi[a, 0, cols, :]) + dot(
            mix[1], wi[a, 1, cols, :]
        )
    for a, got in ((y, got_y), (1 - y, got_n)):
        work[a, :, lanes((1 - c) * width, width)] = dot(mix[0], got[0]) + dot(mix[1], got[1])
    split_sum(ids, work, kept, sent)


def qkv_back_kernel(ids, grad, w_own, got_y, got_n, kept, sent, work):
    c, y = ids[1], ids[2]
    width = kept.shape[1] // 2
    for a, got in ((y, got_y), (1 - y, got_n)):
        for b in range(2):
            total = None
            for s in range(3):
                left = grad[:, s * width : (s + 1) * width]
                right = w_own[a, s, :, lanes(c * width, width)] if b == 0 else got[s]
                part = dot(left, right, NT)
                total = part if total is None else total + part
            where = c if b == 0 else 1 - c
            work[a, :, lanes(where * width, width)] = total
    split_sum(ids, work, kept, sent)


def middle_back_kernel(
    ids, g_own, g_got, middle, gain, gd_own, gd_got, wout, wout_got,
    grad_middle, branch_own, attended, gain_grad, work,
):
    r = ids[0]
    half = g_own.shape[1]
    here, there = lanes(r * half, half), lanes((1 - r) * half, half)
    work[:, here] = g_own[...].astype(F32)
    work[:, there] = g_got[...].astype(F32)
    grad_middle[:, here] = gd_own[...].astype(F32)
    grad_middle[:, there] = gd_got[...].astype(F32)
    total = None
    for rows in row_steps(g_own.shape[0]):
        normal, scale = normalize(middle[rows, :])
        grad = work[rows, :]
        grad_middle[rows, :] += norm_backward(grad, normal, scale, gain[...])
        part = jnp.sum(grad * normal, axis=0, keepdims=True)
        total = part if total is None else total + part
    gain_grad[...] = total
    branch_own[...] = grad_middle[:, here].astype(BF)
    other = grad_middle[:, there].astype(BF)
    attended[...] = (
        dot(branch_own[...], wout[r], NT) + dot(other, wout_got[...], NT)
    ).astype(BF)


def input_back_kernel(
    ids, g_own, g_got, hidden, gain, grad_middle, grad_in, gain_grad, work
):
    r, c = ids[0], ids[1]
    half = g_own.shape[1]
    work[:, lanes(r * half, half)] = g_own[...].astype(F32)
    work[:, lanes((1 - r) * half, half)] = g_got[...].astype(F32)
    total = None
    for rows in row_steps(g_own.shape[0]):
        normal, scale = normalize(hidden[rows, :].astype(F32))
        grad = work[rows, :]
        work[rows, :] = grad_middle[rows, :] + norm_backward(grad, normal, scale, gain[...])
        part = jnp.sum(grad * normal, axis=0, keepdims=True)
        total = part if total is None else total + part
    gain_grad[...] = total
    width = half // 2
    split_lanes(grad_in, 0, 0, g_own.shape[0], width // 128, work[:, block(r, c, width)])


def last_kernel(
    ids, normed, proj, att_own, att_got, branch, kept_own, sent_own, kept_far, sent_far
):
    r, c, y = ids[0], ids[1], ids[2]
    count, rows = kept_own.shape[0], kept_own.shape[1]
    side = proj.shape[1]
    for a, near, far in ((y, kept_own, kept_far), (1 - y, sent_own, sent_far)):
        for b, out in ((c, near), (1 - c, far)):
            width = att_own.shape[1]
            total = dot(normed[:, block(a, b, width)], proj[...], TN).astype(BF)
            for j in range(count):
                out[j, :, :side] = total[j * rows : (j + 1) * rows]
        left = jnp.where(r == a, att_own[...], att_got[...])
        total = dot(left, branch[...], TN).astype(BF)
        for j in range(count):
            near[j, :, side:] = total[j * rows : (j + 1) * rows]


def merged(place, first, second):
    count = first.shape[0]
    for m in range(count):
        yield place ^ m, first, m
        yield place ^ (m + count), second, m


def split_lanes(out, rows, start, count, per, value):
    for t in range(value.shape[1] // 128):
        out[pl.ds(rows * per + start + t, count, stride=per), :] = value[
            :, t * 128 : (t + 1) * 128
        ].astype(F32)


def wi_out_kernel(ids, own_first, own_second, far_first, far_second, out):
    c = ids[1]
    size = own_first.shape[1]
    hid = out.shape[2] // 2
    parts = own_first.shape[0] // 2
    for where, base, refs in (
        (c, ids[3], (own_first, own_second)),
        (1 - c, ids[5], (far_first, far_second)),
    ):
        for place, ref, m in merged(base, *refs):
            a, g, j = place // (2 * parts), (place // parts) % 2, place % parts
            start = where * hid + jnp.minimum(j * size, hid - size)
            out[a, g, pl.ds(pl.multiple_of(start, 16), size), :] = ref[m].astype(F32)


def wo_out_kernel(hid, ids, first, second, out):
    size, width = first.shape[1], first.shape[2]
    parts = first.shape[0] // 2
    per = 2 * width // 128
    for place, ref, m in merged(ids[5], first, second):
        l, a, j = place // (2 * parts), (place // parts) % 2, place % parts
        row = a * hid + jnp.minimum(j * size, hid - size)
        split_lanes(out, row, l * (per // 2), size, per, ref[m])


def last_out_kernel(ids, own_first, own_second, far_first, far_second, qkv, wout):
    c = ids[1]
    size = own_first.shape[1]
    side = far_first.shape[2]
    width = side // 3
    per = 2 * width // 128
    for where, refs in ((c, (own_first, own_second)), (1 - c, (far_first, far_second))):
        for place, ref, m in merged(ids[3], *refs):
            row = place * size
            for s in range(3):
                value = ref[m, :, s * width : (s + 1) * width]
                split_lanes(
                    qkv, row, s * per + where * (per // 2), size, 3 * per, value
                )
            if ref.shape[2] > side:
                split_lanes(wout, row, 0, size, per, ref[m, :, side:])


def stream(kept, sent, order, cross):
    index = lax.axis_index("dp")
    for bit, after in zip(order, order[1:]):
        got = yield sent, bit
        mine = lax.bitwise_and(index, after) != 0
        half = kept.shape[0] // 2
        ks, gs = (kept[:half], kept[half:]), (got[:half], got[half:])
        low, high = [(k.astype(F32) + g.astype(F32)).astype(BF) for k, g in zip(ks, gs)]
        sent = jnp.where(mine, low, high)
        kept = jnp.where(mine, high, low)
    got = yield sent, order[-1]
    value = (kept.astype(F32) + got.astype(F32)).astype(BF)
    if cross:
        value = yield value, "col"
    for bit in order[:0:-1]:
        got = yield value, bit
        value = jnp.concatenate([value, got], axis=0)
    got = yield value, order[0]
    return value, got


def small_stream(value, order):
    for bit in order:
        got = yield value, bit
        value = value + got
    return value


def group_sum(kept, sent):
    half = (kept + swap(sent, "row").astype(F32)).astype(BF)
    got = yield half, "col"
    half = (half.astype(F32) + got.astype(F32)).astype(BF)
    return half, swap(half, "row")


def group_steps(kept, sent):
    got = yield sent, "row"
    half = (kept + got.astype(F32)).astype(BF)
    got = yield half, "col"
    half = (half.astype(F32) + got.astype(F32)).astype(BF)
    got = yield half, "row"
    return half, got


class Streams:
    def __init__(self):
        self.work, self.flight, self.done, self.token = {}, {}, {}, None

    def step(self, name, got):
        try:
            value, way = self.work[name].send(got)
        except StopIteration as end:
            self.done[name] = end.value
            self.token = jax.tree.leaves(end.value)[0]
            return
        self.token = value
        self.flight[name] = swap(value, way) if isinstance(way, str) else dp_swap(value, way)

    def add(self, name, steps):
        self.work[name] = steps
        self.step(name, None)

    def run(self, names):
        for name in names:
            self.step(name, self.after(self.flight.pop(name)))

    def after(self, value):
        return lax.optimization_barrier((value, self.token))[0]


def place_of(order):
    index = lax.axis_index("dp").astype(jnp.int32)
    place = jnp.int32(0)
    for bit in order:
        place = 2 * place + (lax.bitwise_and(index, bit) != 0).astype(jnp.int32)
    return place


def shards(hidden_in, doc_lens, norm1_gain, wqkv, wout, norm2_gain, wi, wo, out_grad):
    tokens, _, width = hidden_in.shape
    half, full = 2 * width, 4 * width
    hid = wo.shape[1]
    count = lax.axis_size("dp")
    row, col = lax.axis_index("row"), lax.axis_index("col")
    side = lax.bitwise_and(lax.axis_index("dp"), 1)
    order = bits_of(count)
    ends = jnp.cumsum(doc_lens[0])
    other = order[1:2] + order[:1] + order[2:]
    bit = (lax.bitwise_and(lax.axis_index("dp"), other[0]) != 0).astype(jnp.int32)
    head = [row, col, side, place_of(order), bit, place_of(other)]
    ids = jnp.concatenate([jnp.stack([h.astype(jnp.int32) for h in head]), ends])

    places = jnp.arange(tokens, dtype=jnp.int32)
    passed = ends[None, :] <= places[:, None]
    doc_start = jnp.sum(jnp.where(passed, doc_lens[0][None, :], 0), axis=1)
    occupied = (places < ends[-1]).astype(BF)[:, None]
    frequency = jnp.exp(
        jnp.arange(HD // 2, dtype=F32) * (-2.0 * math.log(ROPE_BASE) / HD)
    )
    angles = (places - doc_start).astype(F32)[:, None] * frequency[None, :]
    tables = lax.optimization_barrier((jnp.cos(angles), jnp.sin(angles)))
    cosine, sine = [jnp.tile(t, (1, 2 * width // HD)) for t in tables]

    own = hidden_in[:, 0, :]
    own_x = swap(own, "col")
    others = swap(jnp.stack([own, own_x]), "row")
    gains = jnp.concatenate([norm1_gain, norm2_gain], axis=0)
    gains = ordered(col, gains, swap(gains, "col"), 1)
    gains = ordered(row, gains, swap(gains, "row"), 1)
    gain_one, gain_two = gains[0:1], gains[1:2]

    w_qkv = wqkv.transpose(0, 2, 3, 1, 4).reshape(2, 3, width, half)
    qkv_send = lax.dynamic_slice(
        w_qkv, (side, 0, 0, (1 - col) * width), (1, 3, width, width)
    )[0]
    qkv_y = swap(qkv_send, "col")
    qkv_n = dp_swap(qkv_y, 1)
    w_in = wi.transpose(0, 2, 3, 4, 1).reshape(2, 2, 2 * hid, width)
    in_send = lax.dynamic_slice(
        w_in, (side, 0, (1 - col) * hid, 0), (1, 2, hid, width)
    )[0]
    grad_own = out_grad[:, 0, :] * occupied
    in_send, grad_own, qkv_y = lax.optimization_barrier((in_send, grad_own, qkv_y))
    in_y = swap(in_send, "col")
    w_down = wo.reshape(2, hid, half)
    down_got = swap(lax.dynamic_index_in_dim(w_down, 1 - row, 0, False), "row")
    w_out = wout.reshape(2, width, half)
    out_got = swap(lax.dynamic_index_in_dim(w_out, 1 - row, 0, False), "row")

    qkv_n, down_got, out_got = lax.optimization_barrier((qkv_n, down_got, out_got))

    grad_x = swap(grad_own, "col")

    hidden, normed_one = call(
        norm_kernel,
        (((tokens, full), BF), ((tokens, full), BF)),
        ids, own, own_x, others, gain_one,
    )
    qkv, attended, probs = call(
        attend_kernel,
        (((tokens, 3 * width), BF), ((tokens, width), BF), ((width // HD, tokens, tokens), BF)),
        ids, normed_one, w_qkv, qkv_y, qkv_n, cosine, sine,
    )
    attended, in_y, grad_x = lax.optimization_barrier((attended, in_y, grad_x))
    in_n = dp_swap(in_y, 1)
    grad_half = ordered(col, grad_own, grad_x, 1)
    grad_other = swap(grad_half, "row")
    attended_got = swap(attended, "row")
    (branch,) = call(
        branch_kernel, (((tokens, half), BF),), ids, attended, attended_got, w_out,
    )
    branch = (branch.astype(F32) + swap(branch, "col").astype(F32)).astype(BF)
    branch_got = swap(branch, "row")

    wide = -(-hid // 128) * 128
    middle, normed_two, activated, mix = call(
        ffn_kernel,
        (
            ((tokens, full), F32), ((tokens, full), BF), ((tokens, wide), BF),
            ((2, tokens, hid), BF),
        ),
        ids, hidden, branch, branch_got, gain_two, w_in, in_y, in_n, grad_half, grad_other,
        w_down, down_got,
    )
    parts = max(count // 4, 1)
    size, _ = pieces(hid, parts)
    streams = Streams()
    blocks = (count // 2, size, width)
    halves = [
        part.reshape(blocks)
        for part in call(
            wi_kernel, (((2, parts, size, width), BF),) * 4, ids, mix, normed_two
        )
    ]
    streams.add("W1", stream(halves[0], halves[1], order, False))
    kept, sent = call(
        ffn_back_kernel,
        (((tokens, half), F32), ((tokens, half), BF)),
        ids, streams.after(mix), w_in, in_y, in_n,
        scratch=[pltpu.VMEM((2, tokens, half), F32)],
    )
    streams.add("C", group_sum(kept, sent))
    activated_got = swap(activated, "row")
    kept, sent = call(
        functools.partial(wo_kernel, hid), (((2, parts, size, width), BF),) * 2,
        ids, activated, streams.after(activated_got), grad_half,
    )
    streams.add("O", stream(kept.reshape(blocks), sent.reshape(blocks), other, False))
    streams.add("W2", stream(halves[2], halves[3], other, True))
    streams.run(["W1", "O", "C"])
    two_own, two_got = streams.done["C"]
    grad_middle, branch_grad, grad_attended, gain_two_grad = call(
        middle_back_kernel,
        (
            ((tokens, full), F32), ((tokens, half), BF), ((tokens, width), BF), ((1, full), F32),
        ),
        ids, two_own, two_got, middle, gain_two, grad_half, grad_other, w_out, out_got,
        scratch=[pltpu.VMEM((tokens, full), F32)],
    )
    (grad_proj,) = call(
        attend_back_kernel,
        (((tokens, 3 * width), BF),),
        ids, qkv, probs, grad_attended, cosine, sine,
    )
    rows = half // count
    near, far = (count // 2, rows, 3 * width + half), (count // 2, rows, 3 * width)
    halves = call(
        last_kernel, ((near, BF), (near, BF), (far, BF), (far, BF)),
        ids, normed_one, grad_proj, attended, attended_got, branch_grad,
    )
    streams.add("L2", stream(halves[2], halves[3], order, True))
    streams.add("L1", stream(halves[0], halves[1], order, False))
    kept, sent = call(
        qkv_back_kernel,
        (((tokens, half), F32), ((tokens, half), BF)),
        ids, streams.after(grad_proj), w_qkv, qkv_y, qkv_n,
        scratch=[pltpu.VMEM((2, tokens, half), F32)],
    )
    streams.add("D", group_steps(kept, sent))
    for _ in range(3):
        streams.run(["O", "W1", "W2", "L2", "L1", "D"])
    one_own, one_got = streams.done["D"]
    grad_in, gain_one_grad = call(
        input_back_kernel,
        (((tokens * width // 128, 128), F32), ((1, full), F32)),
        ids, one_own, one_got, hidden, gain_one, grad_middle,
        scratch=[pltpu.VMEM((tokens, full), F32)],
    )
    mine = 2 * row + col
    small = jnp.concatenate([pick(gain_one_grad, mine, 4, 1), pick(gain_two_grad, mine, 4, 1)])
    kept, sent = call(
        down_kernel,
        (((tokens, width), F32), ((tokens, width), BF)),
        ids, activated, streams.after(activated_got), w_down, middle,
    )
    hidden_out = (kept + swap(sent, "col").astype(F32)).astype(BF)
    streams.add("G", small_stream(small, order))
    if len(order) == 3:
        streams.run(LATE)
    else:
        while streams.flight:
            streams.run(list(streams.flight))
    own_first, own_second = streams.done["W1"]
    far_first, far_second = streams.done["W2"]
    (grad_wi,) = call(
        wi_out_kernel, (((2, 2, 2 * hid, width), F32),),
        ids, own_first, own_second, far_first, far_second,
    )
    grad_wi = grad_wi.reshape(2, 2, 1, 2 * hid, width).transpose(0, 4, 1, 2, 3)
    (grad_wo,) = call(
        functools.partial(wo_out_kernel, hid), (((2 * hid * half // 128, 128), F32),),
        ids, *streams.done["O"],
    )
    grad_wqkv, grad_wout = call(
        last_out_kernel,
        (((half * 3 * half // 128, 128), F32), ((half * half // 128, 128), F32)),
        ids, *streams.done["L1"], *streams.done["L2"],
    )
    small = streams.done["G"]
    return (
        hidden_out[:, None, :],
        grad_in.reshape(tokens, 1, width),
        small[0:1],
        grad_wqkv.reshape(2, width, 3, 1, half),
        grad_wout.reshape(wout.shape),
        small[1:2],
        grad_wi,
        grad_wo.reshape(wo.shape),
    )


def solution(mesh):
    return jax.shard_map(
        shards,
        mesh=mesh,
        in_specs=(
            P("dp", "row", "col"),
            P("dp", None),
            P("row", "col"),
            P(None, "col", None, "row", None),
            P(None, "col", "row", None),
            P("row", "col"),
            P(None, "col", None, "row", None),
            P(None, "col", "row", None),
            P("dp", "row", "col"),
        ),
        out_specs=(
            P("dp", "row", "col"),
            P("dp", "row", "col"),
            P("row", "col"),
            P(None, "col", None, "row", None),
            P(None, "col", "row", None),
            P("row", "col"),
            P(None, "col", None, "row", None),
            P(None, "col", "row", None),
        ),
        check_vma=False,
    )
```

```python
import functools
import math

import jax
import jax.numpy as jnp
from jax import lax
from jax.experimental import pallas as pl
from jax.experimental.pallas import tpu as pltpu
from jax.sharding import PartitionSpec as P

HD = 64
EPSILON = 1e-05
ROPE_BASE = 160000.0
F32 = jnp.float32
BF = jnp.bfloat16
LATE = (
    "W2", "L2", "L1", "G", "W1", "W2", "G", "L2", "L1", "G", "O", "W2", "W1", "L2",
)
NN = ((1,), (0,))
NT = ((1,), (1,))
TN = ((0,), (0,))


def dot(left, right, dims=NN):
    return lax.dot_general(left, right, (dims, ((), ())), preferred_element_type=F32)


def swap(value, axis):
    return lax.ppermute(value, axis, [(0, 1), (1, 0)])


def dp_swap(value, bit):
    size = lax.axis_size("dp")
    return lax.ppermute(value, "dp", [(i, i ^ bit) for i in range(size)])


def ordered(index, mine, other, axis):
    return jnp.where(
        index == 0,
        jnp.concatenate([mine, other], axis),
        jnp.concatenate([other, mine], axis),
    )


def pick(value, index, parts, axis):
    size = value.shape[axis] // parts
    return lax.dynamic_slice_in_dim(value, index * size, size, axis)


def bits_of(size):
    assert size & (size - 1) == 0
    return [1 << k for k in range(size.bit_length() - 1)]


def call(kernel, outs, ids, *args, scratch=(), flops=1024):
    outs = tuple(jax.ShapeDtypeStruct(s, d) for s, d in outs)
    vmem = pl.BlockSpec(memory_space=pltpu.VMEM)
    return pl.pallas_call(
        kernel,
        out_shape=outs,
        in_specs=[pl.BlockSpec(memory_space=pltpu.SMEM)] + [vmem] * len(args),
        out_specs=tuple(vmem for _ in outs),
        scratch_shapes=list(scratch),
        compiler_params=pltpu.CompilerParams(vmem_limit_bytes=36 * 2**20),
        cost_estimate=pl.CostEstimate(
            flops=flops, bytes_accessed=1024, transcendentals=0
        ),
    )(ids, *args)


def lanes(start, size):
    return pl.ds(pl.multiple_of(start, size), size)


def block(a, b, width):
    return lanes((2 * a + b) * width, width)


def normalize(values):
    centred = values - jnp.mean(values, axis=1, keepdims=True)
    scale = lax.rsqrt(jnp.mean(centred * centred, axis=1, keepdims=True) + EPSILON)
    return (centred * scale, scale)


def norm_backward(grad, normal, scale, gain):
    hat = grad * gain
    correction = (
        hat
        - jnp.mean(hat, axis=1, keepdims=True)
        - normal * jnp.mean(hat * normal, axis=1, keepdims=True)
    )
    return scale * correction


def row_steps(count):
    step = 128 if count % 128 == 0 else count
    return [pl.ds(i, step) for i in range(0, count, step)]


def norm_kernel(ids, own, own_x, others, gain, hidden, normed):
    r, c = ids[0], ids[1]
    width = own.shape[1]
    hidden[:, block(r, c, width)] = own[...]
    hidden[:, block(r, 1 - c, width)] = own_x[...]
    hidden[:, block(1 - r, c, width)] = others[0]
    hidden[:, block(1 - r, 1 - c, width)] = others[1]
    for rows in row_steps(own.shape[0]):
        normal, _ = normalize(hidden[rows, :].astype(F32))
        normed[rows, :] = (normal * gain[...]).astype(BF)


def turn(values, lane):
    size = values.shape[1]
    half = HD // 2
    return jnp.where(
        lane % HD < half, -pltpu.roll(values, size - half, 1), pltpu.roll(values, half, 1)
    )


def segments(ids, shape, axis):
    places = lax.broadcasted_iota(jnp.int32, shape, axis)
    total = jnp.zeros(shape, jnp.int32)
    for j in range(6, ids.shape[0]):
        total = total + (places >= ids[j]).astype(jnp.int32)
    return total


def attend_kernel(ids, normed, w_own, got_y, got_n, cosine, sine, qkv, attended, probs):
    c, y = ids[1], ids[2]
    tokens = normed.shape[0]
    width = got_y.shape[2]
    lane = lax.broadcasted_iota(jnp.int32, (tokens, width), 1)

    def wide(table):
        return jnp.concatenate([table[...]] * (width // table.shape[1]), axis=1)

    for s in range(3):
        total = None
        for a, got in ((y, got_y), (1 - y, got_n)):
            part = dot(normed[:, block(a, c, width)], w_own[a, s, :, lanes(c * width, width)])
            part += dot(normed[:, block(a, 1 - c, width)], got[s])
            total = part if total is None else total + part
        if s < 2:
            total = total * wide(cosine) + turn(total, lane) * wide(sine)
        qkv[:, s * width : (s + 1) * width] = total.astype(BF)
    pair = 2 * HD
    factor = HD**-0.5
    keys_segment = segments(ids, (1, tokens), 1)
    step = min(256, tokens)
    for start in range(0, tokens, step):
        rows = slice(start, start + step)
        same = (segments(ids, (tokens, 1), 0)[rows]) == keys_segment
        low = lax.broadcasted_iota(jnp.int32, (step, pair), 1) < HD
        for h in range(0, width, pair):
            query = qkv[rows, h : h + pair]
            key = qkv[:, width + h : width + h + pair]
            value = qkv[:, 2 * width + h : 2 * width + h + pair]
            results = []
            for side in range(2):
                mine = low if side == 0 else jnp.logical_not(low)
                scores = dot(jnp.where(mine, query, jnp.zeros_like(query)), key, NT) * factor
                scores = jnp.where(same, scores, -1e30)
                raised = jnp.exp(scores - jnp.max(scores, axis=1, keepdims=True))
                weights = (raised / jnp.sum(raised, axis=1, keepdims=True)).astype(BF)
                probs[h // HD + side, rows, :] = weights
                results.append(dot(weights, value))
            attended[rows, h : h + pair] = jnp.where(low, results[0], results[1]).astype(BF)


def attend_back_kernel(ids, qkv, probs, grad, cosine, sine, out):
    tokens = qkv.shape[0]
    width = qkv.shape[1] // 3
    pair = 2 * HD
    factor = HD**-0.5
    low = lax.broadcasted_iota(jnp.int32, (tokens, pair), 1) < HD
    lane = lax.broadcasted_iota(jnp.int32, (tokens, pair), 1)
    for h in range(0, width, pair):
        query = qkv[:, h : h + pair]
        key = qkv[:, width + h : width + h + pair]
        value = qkv[:, 2 * width + h : 2 * width + h + pair]
        top = grad[:, h : h + pair]
        parts = []
        for side in range(2):
            mine = low if side == 0 else jnp.logical_not(low)
            weights = probs[h // HD + side]
            grad_values = dot(weights, top, TN)
            grad_probs = dot(jnp.where(mine, top, jnp.zeros_like(top)), value, NT)
            wide = weights.astype(F32)
            product = wide * grad_probs
            grad_scores = (product - wide * jnp.sum(product, axis=1, keepdims=True)).astype(BF)
            parts.append(
                (
                    dot(grad_scores, key) * factor,
                    dot(grad_scores, query, TN) * factor,
                    grad_values,
                )
            )
        for s in range(3):
            total = jnp.where(low, parts[0][s], parts[1][s])
            if s < 2:
                total = total * cosine[...] - turn(total, lane) * sine[...]
            out[:, s * width + h : s * width + h + pair] = total.astype(BF)


def branch_kernel(ids, own, other, wout, out):
    r = ids[0]
    out[...] = (dot(own[...], wout[r]) + dot(other[...], wout[1 - r])).astype(BF)


def ffn_kernel(
    ids, hidden, br_own, br_got, gain, wi, got_y, got_n, gd_own, gd_got, wo, wo_got,
    middle, normed, activated, mix,
):
    r, c, y = ids[0], ids[1], ids[2]
    half = br_own.shape[1]
    width = half // 2
    hid = mix.shape[2]
    here, there = lanes(r * half, half), lanes((1 - r) * half, half)
    middle[:, here] = hidden[:, here].astype(F32) + br_own[...].astype(F32)
    middle[:, there] = hidden[:, there].astype(F32) + br_got[...].astype(F32)
    for rows in row_steps(hidden.shape[0]):
        normal, _ = normalize(middle[rows, :])
        normed[rows, :] = (normal * gain[...]).astype(BF)
    cols = pl.ds(pl.multiple_of(c * hid, 16), hid)
    step = 256
    for start in range(0, hidden.shape[0], step):
        rows = pl.ds(start, step)
        parts = []
        for g in range(2):
            total = dot(normed[rows, block(0, c, width)], wi[0, g, cols, :], NT)
            total += dot(normed[rows, block(1, c, width)], wi[1, g, cols, :], NT)
            total += dot(normed[rows, block(y, 1 - c, width)], got_y[g], NT)
            total += dot(normed[rows, block(1 - y, 1 - c, width)], got_n[g], NT)
            parts.append(total)
        gate, up = parts
        grad = dot(gd_own[rows, :], wo[r], NT) + dot(gd_got[rows, :], wo_got[...], NT)
        cdf = 0.5 + 0.5 * lax.erf(gate * (0.5**0.5))
        pdf = jnp.exp(-0.5 * gate * gate) * ((2.0 * math.pi) ** -0.5)
        gelu = gate * cdf
        activated[rows, :hid] = (gelu * up).astype(BF)
        mix[0, rows, :] = (grad * up * (cdf + gate * pdf)).astype(BF)
        mix[1, rows, :] = (grad * gelu).astype(BF)


def pieces(count, parts):
    size = -(-count // (16 * parts)) * 16
    return size, [min(j * size, count - size) for j in range(parts)]


def wi_kernel(ids, mix, normed, kept_own, sent_own, kept_far, sent_far):
    c, y, z = ids[1], ids[2], ids[4]
    width = normed.shape[1] // 4
    size, starts = pieces(mix.shape[2], kept_own.shape[1])
    outs = (kept_own, sent_own, kept_far, sent_far)
    places = ((y, c), (1 - y, c), (z, 1 - c), (1 - z, 1 - c))
    right = jnp.concatenate([normed[:, block(a, b, width)] for a, b in places], axis=1)
    for g in range(2):
        total = dot(mix[g], right, TN).astype(BF)
        for k, out in enumerate(outs):
            for j, start in enumerate(starts):
                out[g, j] = total[start : start + size, k * width : (k + 1) * width]


def wo_kernel(hid, ids, own, other, down, kept, sent):
    r, y = ids[0], ids[4]
    width = down.shape[1] // 2
    size, starts = pieces(hid, kept.shape[1])
    right = jnp.concatenate([down[:, lanes(l * width, width)] for l in (y, 1 - y)], axis=1)
    for a, ref in ((r, own), (1 - r, other)):
        total = dot(ref[:, :hid], right, TN).astype(BF)
        for k, out in enumerate((kept, sent)):
            for j, start in enumerate(starts):
                out[a, j] = total[start : start + size, k * width : (k + 1) * width]


def down_kernel(ids, own, other, wo, middle, kept, sent):
    r, c = ids[0], ids[1]
    width = kept.shape[1]
    hid = wo.shape[1]
    for b, ref in ((c, kept), (1 - c, sent)):
        cols = lanes(b * width, width)
        total = dot(own[:, :hid], wo[r, :, cols]) + dot(other[:, :hid], wo[1 - r, :, cols])
        if ref is kept:
            total = total + middle[:, block(r, c, width)]
        ref[...] = total.astype(ref.dtype)


def split_sum(ids, work, kept, sent):
    r = ids[0]
    kept[...] = work[r]
    sent[...] = work[1 - r].astype(BF)


def ffn_back_kernel(ids, mix, wi, got_y, got_n, kept, sent, work):
    c, y = ids[1], ids[2]
    width = kept.shape[1] // 2
    hid = mix.shape[2]
    cols = pl.ds(pl.multiple_of(c * hid, 16), hid)
    for a in range(2):
        work[a, :, lanes(c * width, width)] = dot(mix[0], wi[a, 0, cols, :]) + dot(
            mix[1], wi[a, 1, cols, :]
        )
    for a, got in ((y, got_y), (1 - y, got_n)):
        work[a, :, lanes((1 - c) * width, width)] = dot(mix[0], got[0]) + dot(mix[1], got[1])
    split_sum(ids, work, kept, sent)


def qkv_back_kernel(ids, grad, w_own, got_y, got_n, kept, sent, work):
    c, y = ids[1], ids[2]
    width = kept.shape[1] // 2
    for a, got in ((y, got_y), (1 - y, got_n)):
        for b in range(2):
            total = None
            for s in range(3):
                left = grad[:, s * width : (s + 1) * width]
                right = w_own[a, s, :, lanes(c * width, width)] if b == 0 else got[s]
                part = dot(left, right, NT)
                total = part if total is None else total + part
            where = c if b == 0 else 1 - c
            work[a, :, lanes(where * width, width)] = total
    split_sum(ids, work, kept, sent)


def middle_back_kernel(
    ids, g_own, g_got, middle, gain, gd_own, gd_got, wout, wout_got,
    grad_middle, branch_own, attended, gain_grad, work,
):
    r = ids[0]
    half = g_own.shape[1]
    here, there = lanes(r * half, half), lanes((1 - r) * half, half)
    work[:, here] = g_own[...].astype(F32)
    work[:, there] = g_got[...].astype(F32)
    grad_middle[:, here] = gd_own[...].astype(F32)
    grad_middle[:, there] = gd_got[...].astype(F32)
    total = None
    for rows in row_steps(g_own.shape[0]):
        normal, scale = normalize(middle[rows, :])
        grad = work[rows, :]
        grad_middle[rows, :] += norm_backward(grad, normal, scale, gain[...])
        part = jnp.sum(grad * normal, axis=0, keepdims=True)
        total = part if total is None else total + part
    gain_grad[...] = total
    branch_own[...] = grad_middle[:, here].astype(BF)
    other = grad_middle[:, there].astype(BF)
    attended[...] = (
        dot(branch_own[...], wout[r], NT) + dot(other, wout_got[...], NT)
    ).astype(BF)


def input_back_kernel(
    ids, g_own, g_got, hidden, gain, grad_middle, grad_in, gain_grad, work
):
    r, c = ids[0], ids[1]
    half = g_own.shape[1]
    work[:, lanes(r * half, half)] = g_own[...].astype(F32)
    work[:, lanes((1 - r) * half, half)] = g_got[...].astype(F32)
    total = None
    for rows in row_steps(g_own.shape[0]):
        normal, scale = normalize(hidden[rows, :].astype(F32))
        grad = work[rows, :]
        work[rows, :] = grad_middle[rows, :] + norm_backward(grad, normal, scale, gain[...])
        part = jnp.sum(grad * normal, axis=0, keepdims=True)
        total = part if total is None else total + part
    gain_grad[...] = total
    width = half // 2
    split_lanes(grad_in, 0, 0, g_own.shape[0], width // 128, work[:, block(r, c, width)])


def last_kernel(
    ids, normed, proj, att_own, att_got, branch, kept_own, sent_own, kept_far, sent_far
):
    r, c, y = ids[0], ids[1], ids[2]
    count, rows = kept_own.shape[0], kept_own.shape[1]
    side = proj.shape[1]
    for a, near, far in ((y, kept_own, kept_far), (1 - y, sent_own, sent_far)):
        for b, out in ((c, near), (1 - c, far)):
            width = att_own.shape[1]
            total = dot(normed[:, block(a, b, width)], proj[...], TN).astype(BF)
            for j in range(count):
                out[j, :, :side] = total[j * rows : (j + 1) * rows]
        left = jnp.where(r == a, att_own[...], att_got[...])
        total = dot(left, branch[...], TN).astype(BF)
        for j in range(count):
            near[j, :, side:] = total[j * rows : (j + 1) * rows]


def merged(place, first, second):
    count = first.shape[0]
    for m in range(count):
        yield place ^ m, first, m
        yield place ^ (m + count), second, m


def split_lanes(out, rows, start, count, per, value):
    for t in range(value.shape[1] // 128):
        out[pl.ds(rows * per + start + t, count, stride=per), :] = value[
            :, t * 128 : (t + 1) * 128
        ].astype(F32)


def wi_out_kernel(ids, own_first, own_second, far_first, far_second, out):
    c = ids[1]
    size = own_first.shape[1]
    hid = out.shape[2] // 2
    parts = own_first.shape[0] // 2
    for where, base, refs in (
        (c, ids[3], (own_first, own_second)),
        (1 - c, ids[5], (far_first, far_second)),
    ):
        for place, ref, m in merged(base, *refs):
            a, g, j = place // (2 * parts), (place // parts) % 2, place % parts
            start = where * hid + jnp.minimum(j * size, hid - size)
            out[a, g, pl.ds(pl.multiple_of(start, 16), size), :] = ref[m].astype(F32)


def wo_out_kernel(hid, ids, first, second, out):
    size, width = first.shape[1], first.shape[2]
    parts = first.shape[0] // 2
    per = 2 * width // 128
    for place, ref, m in merged(ids[5], first, second):
        l, a, j = place // (2 * parts), (place // parts) % 2, place % parts
        row = a * hid + jnp.minimum(j * size, hid - size)
        split_lanes(out, row, l * (per // 2), size, per, ref[m])


def last_out_kernel(ids, own_first, own_second, far_first, far_second, qkv, wout):
    c = ids[1]
    size = own_first.shape[1]
    side = far_first.shape[2]
    width = side // 3
    per = 2 * width // 128
    for where, refs in ((c, (own_first, own_second)), (1 - c, (far_first, far_second))):
        for place, ref, m in merged(ids[3], *refs):
            row = place * size
            for s in range(3):
                value = ref[m, :, s * width : (s + 1) * width]
                split_lanes(
                    qkv, row, s * per + where * (per // 2), size, 3 * per, value
                )
            if ref.shape[2] > side:
                split_lanes(wout, row, 0, size, per, ref[m, :, side:])


def stream(kept, sent, order, cross):
    index = lax.axis_index("dp")
    for bit, after in zip(order, order[1:]):
        got = yield sent, bit
        mine = lax.bitwise_and(index, after) != 0
        half = kept.shape[0] // 2
        ks, gs = (kept[:half], kept[half:]), (got[:half], got[half:])
        low, high = [(k.astype(F32) + g.astype(F32)).astype(BF) for k, g in zip(ks, gs)]
        sent = jnp.where(mine, low, high)
        kept = jnp.where(mine, high, low)
    got = yield sent, order[-1]
    value = (kept.astype(F32) + got.astype(F32)).astype(BF)
    if cross:
        value = yield value, "col"
    for bit in order[:0:-1]:
        got = yield value, bit
        value = jnp.concatenate([value, got], axis=0)
    got = yield value, order[0]
    return value, got


def small_stream(value, order):
    for bit in order:
        got = yield value, bit
        value = value + got
    return value


def group_sum(kept, sent):
    half = (kept + swap(sent, "row").astype(F32)).astype(BF)
    got = yield half, "col"
    half = (half.astype(F32) + got.astype(F32)).astype(BF)
    return half, swap(half, "row")


def group_steps(kept, sent):
    got = yield sent, "row"
    half = (kept + got.astype(F32)).astype(BF)
    got = yield half, "col"
    half = (half.astype(F32) + got.astype(F32)).astype(BF)
    got = yield half, "row"
    return half, got


class Streams:
    def __init__(self):
        self.work, self.flight, self.done, self.token = {}, {}, {}, None

    def step(self, name, got):
        try:
            value, way = self.work[name].send(got)
        except StopIteration as end:
            self.done[name] = end.value
            self.token = jax.tree.leaves(end.value)[0]
            return
        self.token = value
        self.flight[name] = swap(value, way) if isinstance(way, str) else dp_swap(value, way)

    def add(self, name, steps):
        self.work[name] = steps
        self.step(name, None)

    def run(self, names):
        for name in names:
            self.step(name, self.after(self.flight.pop(name)))

    def after(self, value):
        return lax.optimization_barrier((value, self.token))[0]


def place_of(order):
    index = lax.axis_index("dp").astype(jnp.int32)
    place = jnp.int32(0)
    for bit in order:
        place = 2 * place + (lax.bitwise_and(index, bit) != 0).astype(jnp.int32)
    return place


def shards(hidden_in, doc_lens, norm1_gain, wqkv, wout, norm2_gain, wi, wo, out_grad):
    tokens, _, width = hidden_in.shape
    half, full = 2 * width, 4 * width
    hid = wo.shape[1]
    count = lax.axis_size("dp")
    row, col = lax.axis_index("row"), lax.axis_index("col")
    side = lax.bitwise_and(lax.axis_index("dp"), 1)
    order = bits_of(count)
    ends = jnp.cumsum(doc_lens[0])
    other = order[1:2] + order[:1] + order[2:]
    bit = (lax.bitwise_and(lax.axis_index("dp"), other[0]) != 0).astype(jnp.int32)
    head = [row, col, side, place_of(order), bit, place_of(other)]
    ids = jnp.concatenate([jnp.stack([h.astype(jnp.int32) for h in head]), ends])

    places = jnp.arange(tokens, dtype=jnp.int32)
    passed = ends[None, :] <= places[:, None]
    doc_start = jnp.sum(jnp.where(passed, doc_lens[0][None, :], 0), axis=1)
    occupied = (places < ends[-1]).astype(BF)[:, None]
    frequency = jnp.exp(
        jnp.arange(HD // 2, dtype=F32) * (-2.0 * math.log(ROPE_BASE) / HD)
    )
    angles = (places - doc_start).astype(F32)[:, None] * jnp.tile(frequency, 4)[None, :]
    cosine, sine = jnp.cos(angles), jnp.sin(angles)

    own = hidden_in[:, 0, :]
    own_x = swap(own, "col")
    gains = jnp.concatenate([norm1_gain, norm2_gain], axis=0)
    gains, own_x = lax.optimization_barrier((gains, own_x))
    others = swap(jnp.stack([own, own_x]), "row")
    gains = ordered(col, gains, swap(gains, "col"), 1)
    gains = ordered(row, gains, swap(gains, "row"), 1)
    gain_one, gain_two = gains[0:1], gains[1:2]

    w_qkv = wqkv.transpose(0, 2, 3, 1, 4).reshape(2, 3, width, half)
    qkv_send = lax.dynamic_slice(
        w_qkv, (side, 0, 0, (1 - col) * width), (1, 3, width, width)
    )[0]
    qkv_y = swap(qkv_send, "col")
    qkv_n = dp_swap(qkv_y, 1)
    w_in = wi.transpose(0, 2, 3, 4, 1).reshape(2, 2, 2 * hid, width)
    in_send = lax.dynamic_slice(
        w_in, (side, 0, (1 - col) * hid, 0), (1, 2, hid, width)
    )[0]
    grad_own = out_grad[:, 0, :]
    in_send, grad_own, qkv_y = lax.optimization_barrier((in_send, grad_own, qkv_y))
    in_y = swap(in_send, "col")
    w_down = wo.reshape(2, hid, half)
    down_got = swap(lax.dynamic_index_in_dim(w_down, 1 - row, 0, False), "row")
    w_out = wout.reshape(2, width, half)
    out_got = swap(lax.dynamic_index_in_dim(w_out, 1 - row, 0, False), "row")

    qkv_n, down_got, out_got = lax.optimization_barrier((qkv_n, down_got, out_got))

    grad_x = swap(grad_own, "col")

    hidden, normed_one = call(
        norm_kernel,
        (((tokens, full), BF), ((tokens, full), BF)),
        ids, own, own_x, others, gain_one,
    )
    qkv, attended, probs = call(
        attend_kernel,
        (((tokens, 3 * width), BF), ((tokens, width), BF), ((width // HD, tokens, tokens), BF)),
        ids, normed_one, w_qkv, qkv_y, qkv_n, cosine, sine,
    )
    attended, in_y, grad_x = lax.optimization_barrier((attended, in_y, grad_x))
    in_n = dp_swap(in_y, 1)
    grad_half = ordered(col, grad_own, grad_x, 1) * occupied
    grad_other = swap(grad_half, "row")
    attended_got = swap(attended, "row")
    (branch,) = call(
        branch_kernel, (((tokens, half), BF),), ids, attended, attended_got, w_out,
    )
    branch = (branch.astype(F32) + swap(branch, "col").astype(F32)).astype(BF)
    branch_got = swap(branch, "row")

    wide = -(-hid // 128) * 128
    middle, normed_two, activated, mix = call(
        ffn_kernel,
        (
            ((tokens, full), F32), ((tokens, full), BF), ((tokens, wide), BF),
            ((2, tokens, hid), BF),
        ),
        ids, hidden, branch, branch_got, gain_two, w_in, in_y, in_n, grad_half, grad_other,
        w_down, down_got,
    )
    parts = max(count // 4, 1)
    size, _ = pieces(hid, parts)
    streams = Streams()
    blocks = (count // 2, size, width)
    kept, sent = call(
        ffn_back_kernel,
        (((tokens, half), F32), ((tokens, half), BF)),
        ids, mix, w_in, in_y, in_n,
        scratch=[pltpu.VMEM((2, tokens, half), F32)],
    )
    mix, sent = lax.optimization_barrier((mix, sent))
    halves = [
        part.reshape(blocks)
        for part in call(
            wi_kernel, (((2, parts, size, width), BF),) * 4, ids, mix, normed_two
        )
    ]
    streams.add("W1", stream(halves[0], halves[1], order, False))
    streams.add("C", group_sum(kept, sent))
    activated_got = swap(activated, "row")
    kept, sent = call(
        functools.partial(wo_kernel, hid), (((2, parts, size, width), BF),) * 2,
        ids, activated, streams.after(activated_got), grad_half,
    )
    streams.add("O", stream(kept.reshape(blocks), sent.reshape(blocks), other, False))
    streams.add("W2", stream(halves[2], halves[3], other, True))
    streams.run(["W1", "O", "C"])
    two_own, two_got = streams.done["C"]
    grad_middle, branch_grad, grad_attended, gain_two_grad = call(
        middle_back_kernel,
        (
            ((tokens, full), F32), ((tokens, half), BF), ((tokens, width), BF), ((1, full), F32),
        ),
        ids, two_own, two_got, middle, gain_two, grad_half, grad_other, w_out, out_got,
        scratch=[pltpu.VMEM((tokens, full), F32)],
    )
    (grad_proj,) = call(
        attend_back_kernel,
        (((tokens, 3 * width), BF),),
        ids, qkv, probs, grad_attended, cosine, sine,
    )
    rows = half // count
    near, far = (count // 2, rows, 3 * width + half), (count // 2, rows, 3 * width)
    halves = call(
        last_kernel, ((near, BF), (near, BF), (far, BF), (far, BF)),
        ids, normed_one, grad_proj, attended, attended_got, branch_grad,
    )
    streams.add("L2", stream(halves[2], halves[3], order, True))
    streams.add("L1", stream(halves[0], halves[1], order, False))
    kept, sent = call(
        qkv_back_kernel,
        (((tokens, half), F32), ((tokens, half), BF)),
        ids, streams.after(grad_proj), w_qkv, qkv_y, qkv_n,
        scratch=[pltpu.VMEM((2, tokens, half), F32)],
    )
    streams.add("D", group_steps(kept, sent))
    for _ in range(3):
        streams.run(["O", "W1", "W2", "L2", "L1", "D"])
    one_own, one_got = streams.done["D"]
    grad_in, gain_one_grad = call(
        input_back_kernel,
        (((tokens * width // 128, 128), F32), ((1, full), F32)),
        ids, one_own, one_got, hidden, gain_one, grad_middle,
        scratch=[pltpu.VMEM((tokens, full), F32)],
    )
    mine = 2 * row + col
    small = jnp.concatenate([pick(gain_one_grad, mine, 4, 1), pick(gain_two_grad, mine, 4, 1)])
    kept, sent = call(
        down_kernel,
        (((tokens, width), F32), ((tokens, width), BF)),
        ids, activated, streams.after(activated_got), w_down, middle,
    )
    hidden_out = (kept + swap(sent, "col").astype(F32)).astype(BF)
    streams.add("G", small_stream(small, order))
    if len(order) == 3:
        streams.run(LATE)
    else:
        for name in list(streams.flight):
            while name in streams.flight:
                streams.run([name])
    streams.run([name for name in ("O",) if name in streams.flight])
    (grad_wo,) = call(
        functools.partial(wo_out_kernel, hid), (((2 * hid * half // 128, 128), F32),),
        ids, *streams.done["O"],
        flops=8 * 10**9,
    )
    streams.token = grad_wo
    streams.run([name for name in ("W1", "W2") if name in streams.flight])
    (grad_wi,) = call(
        wi_out_kernel, (((2, 2, 2 * hid, width), F32),),
        ids, *streams.done["W1"], *streams.done["W2"],
        flops=8 * 10**9,
    )
    streams.token = grad_wi
    grad_wi = grad_wi.reshape(2, 2, 1, 2 * hid, width).transpose(0, 4, 1, 2, 3)
    streams.run([name for name in ("L1", "L2", "G") if name in streams.flight])
    grad_wqkv, grad_wout = call(
        last_out_kernel,
        (((half * 3 * half // 128, 128), F32), ((half * half // 128, 128), F32)),
        ids, *streams.done["L1"], *streams.done["L2"],
    )
    small = streams.done["G"]
    return (
        hidden_out[:, None, :],
        grad_in.reshape(tokens, 1, width),
        small[0:1],
        grad_wqkv.reshape(2, width, 3, 1, half),
        grad_wout.reshape(wout.shape),
        small[1:2],
        grad_wi,
        grad_wo.reshape(wo.shape),
    )


def solution(mesh):
    return jax.shard_map(
        shards,
        mesh=mesh,
        in_specs=(
            P("dp", "row", "col"),
            P("dp", None),
            P("row", "col"),
            P(None, "col", None, "row", None),
            P(None, "col", "row", None),
            P("row", "col"),
            P(None, "col", None, "row", None),
            P(None, "col", "row", None),
            P("dp", "row", "col"),
        ),
        out_specs=(
            P("dp", "row", "col"),
            P("dp", "row", "col"),
            P("row", "col"),
            P(None, "col", None, "row", None),
            P(None, "col", "row", None),
            P("row", "col"),
            P(None, "col", None, "row", None),
            P(None, "col", "row", None),
        ),
        check_vma=False,
    )
```

```python
import functools
import math

import jax
import jax.numpy as jnp
from jax import lax
from jax.experimental import pallas as pl
from jax.experimental.pallas import tpu as pltpu
from jax.sharding import PartitionSpec as P

HD = 64
EPSILON = 1e-05
ROPE_BASE = 160000.0
F32 = jnp.float32
BF = jnp.bfloat16
LATE = (
    "W1", "W2", "L2", "L1", "G", "W2", "W1", "G", "L2", "L1", "G", "O", "W2", "L2",
)
NN = ((1,), (0,))
NT = ((1,), (1,))
TN = ((0,), (0,))


def dot(left, right, dims=NN):
    return lax.dot_general(left, right, (dims, ((), ())), preferred_element_type=F32)


def swap(value, axis):
    return lax.ppermute(value, axis, [(0, 1), (1, 0)])


def dp_swap(value, bit):
    size = lax.axis_size("dp")
    return lax.ppermute(value, "dp", [(i, i ^ bit) for i in range(size)])


def ordered(index, mine, other, axis):
    return jnp.where(
        index == 0,
        jnp.concatenate([mine, other], axis),
        jnp.concatenate([other, mine], axis),
    )


def pick(value, index, parts, axis):
    size = value.shape[axis] // parts
    return lax.dynamic_slice_in_dim(value, index * size, size, axis)


def bits_of(size):
    assert size & (size - 1) == 0
    return [1 << k for k in range(size.bit_length() - 1)]


def call(kernel, outs, ids, *args, scratch=(), flops=1024):
    outs = tuple(jax.ShapeDtypeStruct(s, d) for s, d in outs)
    vmem = pl.BlockSpec(memory_space=pltpu.VMEM)
    return pl.pallas_call(
        kernel,
        out_shape=outs,
        in_specs=[pl.BlockSpec(memory_space=pltpu.SMEM)] + [vmem] * len(args),
        out_specs=tuple(vmem for _ in outs),
        scratch_shapes=list(scratch),
        compiler_params=pltpu.CompilerParams(vmem_limit_bytes=36 * 2**20),
        cost_estimate=pl.CostEstimate(
            flops=flops, bytes_accessed=1024, transcendentals=0
        ),
    )(ids, *args)


def lanes(start, size):
    return pl.ds(pl.multiple_of(start, size), size)


def block(a, b, width):
    return lanes((2 * a + b) * width, width)


def normalize(values):
    centred = values - jnp.mean(values, axis=1, keepdims=True)
    scale = lax.rsqrt(jnp.mean(centred * centred, axis=1, keepdims=True) + EPSILON)
    return (centred * scale, scale)


def norm_backward(grad, normal, scale, gain):
    hat = grad * gain
    correction = (
        hat
        - jnp.mean(hat, axis=1, keepdims=True)
        - normal * jnp.mean(hat * normal, axis=1, keepdims=True)
    )
    return scale * correction


def row_steps(count):
    step = 128 if count % 128 == 0 else count
    return [pl.ds(i, step) for i in range(0, count, step)]


def norm_kernel(ids, own, own_x, others, gain, hidden, normed):
    r, c = ids[0], ids[1]
    width = own.shape[1]
    hidden[:, block(r, c, width)] = own[...]
    hidden[:, block(r, 1 - c, width)] = own_x[...]
    hidden[:, block(1 - r, c, width)] = others[0]
    hidden[:, block(1 - r, 1 - c, width)] = others[1]
    for rows in row_steps(own.shape[0]):
        normal, _ = normalize(hidden[rows, :].astype(F32))
        normed[rows, :] = (normal * gain[...]).astype(BF)


def turn(values, lane):
    size = values.shape[1]
    half = HD // 2
    return jnp.where(
        lane % HD < half, -pltpu.roll(values, size - half, 1), pltpu.roll(values, half, 1)
    )


def segments(ids, shape, axis):
    places = lax.broadcasted_iota(jnp.int32, shape, axis)
    total = jnp.zeros(shape, jnp.int32)
    for j in range(6, ids.shape[0]):
        total = total + (places >= ids[j]).astype(jnp.int32)
    return total


def attend_kernel(ids, normed, w_own, got_y, got_n, cosine, sine, qkv, attended, probs):
    c, y = ids[1], ids[2]
    tokens = normed.shape[0]
    width = got_y.shape[2]
    lane = lax.broadcasted_iota(jnp.int32, (tokens, width), 1)

    def wide(table):
        return jnp.concatenate([table[...]] * (width // table.shape[1]), axis=1)

    for s in range(3):
        total = None
        for a, got in ((y, got_y), (1 - y, got_n)):
            part = dot(normed[:, block(a, c, width)], w_own[a, s, :, lanes(c * width, width)])
            part += dot(normed[:, block(a, 1 - c, width)], got[s])
            total = part if total is None else total + part
        if s < 2:
            total = total * wide(cosine) + turn(total, lane) * wide(sine)
        qkv[:, s * width : (s + 1) * width] = total.astype(BF)
    pair = 2 * HD
    factor = HD**-0.5
    keys_segment = segments(ids, (1, tokens), 1)
    step = min(256, tokens)
    for start in range(0, tokens, step):
        rows = slice(start, start + step)
        same = (segments(ids, (tokens, 1), 0)[rows]) == keys_segment
        low = lax.broadcasted_iota(jnp.int32, (step, pair), 1) < HD
        for h in range(0, width, pair):
            query = qkv[rows, h : h + pair]
            key = qkv[:, width + h : width + h + pair]
            value = qkv[:, 2 * width + h : 2 * width + h + pair]
            results = []
            for side in range(2):
                mine = low if side == 0 else jnp.logical_not(low)
                scores = dot(jnp.where(mine, query, jnp.zeros_like(query)), key, NT) * factor
                scores = jnp.where(same, scores, -1e30)
                raised = jnp.exp(scores - jnp.max(scores, axis=1, keepdims=True))
                weights = (raised / jnp.sum(raised, axis=1, keepdims=True)).astype(BF)
                probs[h // HD + side, rows, :] = weights
                results.append(dot(weights, value))
            attended[rows, h : h + pair] = jnp.where(low, results[0], results[1]).astype(BF)


def attend_back_kernel(ids, qkv, probs, grad, cosine, sine, out):
    tokens = qkv.shape[0]
    width = qkv.shape[1] // 3
    pair = 2 * HD
    factor = HD**-0.5
    low = lax.broadcasted_iota(jnp.int32, (tokens, pair), 1) < HD
    lane = lax.broadcasted_iota(jnp.int32, (tokens, pair), 1)
    for h in range(0, width, pair):
        query = qkv[:, h : h + pair]
        key = qkv[:, width + h : width + h + pair]
        value = qkv[:, 2 * width + h : 2 * width + h + pair]
        top = grad[:, h : h + pair]
        parts = []
        for side in range(2):
            mine = low if side == 0 else jnp.logical_not(low)
            weights = probs[h // HD + side]
            grad_values = dot(weights, top, TN)
            grad_probs = dot(jnp.where(mine, top, jnp.zeros_like(top)), value, NT)
            wide = weights.astype(F32)
            product = wide * grad_probs
            grad_scores = (product - wide * jnp.sum(product, axis=1, keepdims=True)).astype(BF)
            parts.append(
                (
                    dot(grad_scores, key) * factor,
                    dot(grad_scores, query, TN) * factor,
                    grad_values,
                )
            )
        for s in range(3):
            total = jnp.where(low, parts[0][s], parts[1][s])
            if s < 2:
                total = total * cosine[...] - turn(total, lane) * sine[...]
            out[:, s * width + h : s * width + h + pair] = total.astype(BF)


def branch_kernel(ids, own, other, wout, out):
    r = ids[0]
    out[...] = (dot(own[...], wout[r]) + dot(other[...], wout[1 - r])).astype(BF)


def ffn_kernel(
    ids, hidden, br_own, br_got, gain, wi, got_y, got_n, gd_own, gd_got, wo, wo_got,
    middle, normed, activated, mix,
):
    r, c, y = ids[0], ids[1], ids[2]
    half = br_own.shape[1]
    width = half // 2
    hid = mix.shape[2]
    here, there = lanes(r * half, half), lanes((1 - r) * half, half)
    middle[:, here] = hidden[:, here].astype(F32) + br_own[...].astype(F32)
    middle[:, there] = hidden[:, there].astype(F32) + br_got[...].astype(F32)
    for rows in row_steps(hidden.shape[0]):
        normal, _ = normalize(middle[rows, :])
        normed[rows, :] = (normal * gain[...]).astype(BF)
    cols = pl.ds(pl.multiple_of(c * hid, 16), hid)
    step = 256
    for start in range(0, hidden.shape[0], step):
        rows = pl.ds(start, step)
        parts = []
        for g in range(2):
            total = dot(normed[rows, block(0, c, width)], wi[0, g, cols, :], NT)
            total += dot(normed[rows, block(1, c, width)], wi[1, g, cols, :], NT)
            total += dot(normed[rows, block(y, 1 - c, width)], got_y[g], NT)
            total += dot(normed[rows, block(1 - y, 1 - c, width)], got_n[g], NT)
            parts.append(total)
        gate, up = parts
        grad = dot(gd_own[rows, :], wo[r], NT) + dot(gd_got[rows, :], wo_got[...], NT)
        cdf = 0.5 + 0.5 * lax.erf(gate * (0.5**0.5))
        pdf = jnp.exp(-0.5 * gate * gate) * ((2.0 * math.pi) ** -0.5)
        gelu = gate * cdf
        activated[rows, :hid] = (gelu * up).astype(BF)
        mix[0, rows, :] = (grad * up * (cdf + gate * pdf)).astype(BF)
        mix[1, rows, :] = (grad * gelu).astype(BF)


def pieces(count, parts):
    size = -(-count // (16 * parts)) * 16
    return size, [min(j * size, count - size) for j in range(parts)]


def wi_kernel(ids, mix, normed, kept_own, sent_own, kept_far, sent_far):
    c, y, z = ids[1], ids[2], ids[4]
    width = normed.shape[1] // 4
    size, starts = pieces(mix.shape[2], kept_own.shape[1])
    outs = (kept_own, sent_own, kept_far, sent_far)
    places = ((y, c), (1 - y, c), (z, 1 - c), (1 - z, 1 - c))
    right = jnp.concatenate([normed[:, block(a, b, width)] for a, b in places], axis=1)
    for g in range(2):
        total = dot(mix[g], right, TN).astype(BF)
        for k, out in enumerate(outs):
            for j, start in enumerate(starts):
                out[g, j] = total[start : start + size, k * width : (k + 1) * width]


def wo_kernel(hid, ids, own, other, down, kept, sent):
    r, y = ids[0], ids[4]
    width = down.shape[1] // 2
    size, starts = pieces(hid, kept.shape[1])
    right = jnp.concatenate([down[:, lanes(l * width, width)] for l in (y, 1 - y)], axis=1)
    for a, ref in ((r, own), (1 - r, other)):
        total = dot(ref[:, :hid], right, TN).astype(BF)
        for k, out in enumerate((kept, sent)):
            for j, start in enumerate(starts):
                out[a, j] = total[start : start + size, k * width : (k + 1) * width]


def down_kernel(ids, own, other, wo, middle, kept, sent):
    r, c = ids[0], ids[1]
    width = kept.shape[1]
    hid = wo.shape[1]
    for b, ref in ((c, kept), (1 - c, sent)):
        cols = lanes(b * width, width)
        total = dot(own[:, :hid], wo[r, :, cols]) + dot(other[:, :hid], wo[1 - r, :, cols])
        if ref is kept:
            total = total + middle[:, block(r, c, width)]
        ref[...] = total.astype(ref.dtype)


def split_sum(ids, work, kept, sent):
    r = ids[0]
    kept[...] = work[r]
    sent[...] = work[1 - r].astype(BF)


def ffn_back_kernel(ids, mix, wi, got_y, got_n, kept, sent, work):
    c, y = ids[1], ids[2]
    width = kept.shape[1] // 2
    hid = mix.shape[2]
    cols = pl.ds(pl.multiple_of(c * hid, 16), hid)
    for a in range(2):
        work[a, :, lanes(c * width, width)] = dot(mix[0], wi[a, 0, cols, :]) + dot(
            mix[1], wi[a, 1, cols, :]
        )
    for a, got in ((y, got_y), (1 - y, got_n)):
        work[a, :, lanes((1 - c) * width, width)] = dot(mix[0], got[0]) + dot(mix[1], got[1])
    split_sum(ids, work, kept, sent)


def qkv_back_kernel(ids, grad, w_own, got_y, got_n, kept, sent, work):
    c, y = ids[1], ids[2]
    width = kept.shape[1] // 2
    for a, got in ((y, got_y), (1 - y, got_n)):
        for b in range(2):
            total = None
            for s in range(3):
                left = grad[:, s * width : (s + 1) * width]
                right = w_own[a, s, :, lanes(c * width, width)] if b == 0 else got[s]
                part = dot(left, right, NT)
                total = part if total is None else total + part
            where = c if b == 0 else 1 - c
            work[a, :, lanes(where * width, width)] = total
    split_sum(ids, work, kept, sent)


def middle_back_kernel(
    ids, g_own, g_got, middle, gain, gd_own, gd_got, wout, wout_got,
    grad_middle, branch_own, attended, gain_grad, work,
):
    r = ids[0]
    half = g_own.shape[1]
    here, there = lanes(r * half, half), lanes((1 - r) * half, half)
    work[:, here] = g_own[...].astype(F32)
    work[:, there] = g_got[...].astype(F32)
    grad_middle[:, here] = gd_own[...].astype(F32)
    grad_middle[:, there] = gd_got[...].astype(F32)
    total = None
    for rows in row_steps(g_own.shape[0]):
        normal, scale = normalize(middle[rows, :])
        grad = work[rows, :]
        grad_middle[rows, :] += norm_backward(grad, normal, scale, gain[...])
        part = jnp.sum(grad * normal, axis=0, keepdims=True)
        total = part if total is None else total + part
    gain_grad[...] = total
    branch_own[...] = grad_middle[:, here].astype(BF)
    other = grad_middle[:, there].astype(BF)
    attended[...] = (
        dot(branch_own[...], wout[r], NT) + dot(other, wout_got[...], NT)
    ).astype(BF)


def input_back_kernel(
    ids, g_own, g_got, hidden, gain, grad_middle, grad_in, gain_grad, work
):
    r, c = ids[0], ids[1]
    half = g_own.shape[1]
    work[:, lanes(r * half, half)] = g_own[...].astype(F32)
    work[:, lanes((1 - r) * half, half)] = g_got[...].astype(F32)
    total = None
    for rows in row_steps(g_own.shape[0]):
        normal, scale = normalize(hidden[rows, :].astype(F32))
        grad = work[rows, :]
        work[rows, :] = grad_middle[rows, :] + norm_backward(grad, normal, scale, gain[...])
        part = jnp.sum(grad * normal, axis=0, keepdims=True)
        total = part if total is None else total + part
    gain_grad[...] = total
    width = half // 2
    split_lanes(grad_in, 0, 0, g_own.shape[0], width // 128, work[:, block(r, c, width)])


def last_kernel(
    ids, normed, proj, att_own, att_got, branch, kept_own, sent_own, kept_far, sent_far
):
    r, c, y = ids[0], ids[1], ids[2]
    count, rows = kept_own.shape[0], kept_own.shape[1]
    side = proj.shape[1]
    for a, near, far in ((y, kept_own, kept_far), (1 - y, sent_own, sent_far)):
        for b, out in ((c, near), (1 - c, far)):
            width = att_own.shape[1]
            total = dot(normed[:, block(a, b, width)], proj[...], TN).astype(BF)
            for j in range(count):
                out[j, :, :side] = total[j * rows : (j + 1) * rows]
        left = jnp.where(r == a, att_own[...], att_got[...])
        total = dot(left, branch[...], TN).astype(BF)
        for j in range(count):
            near[j, :, side:] = total[j * rows : (j + 1) * rows]


def merged(place, first, second):
    count = first.shape[0]
    for m in range(count):
        yield place ^ m, first, m
        yield place ^ (m + count), second, m


def split_lanes(out, rows, start, count, per, value):
    for t in range(value.shape[1] // 128):
        out[pl.ds(rows * per + start + t, count, stride=per), :] = value[
            :, t * 128 : (t + 1) * 128
        ].astype(F32)


def wi_out_kernel(ids, own_first, own_second, far_first, far_second, out):
    c = ids[1]
    size = own_first.shape[1]
    hid = out.shape[2] // 2
    parts = own_first.shape[0] // 2
    for where, base, refs in (
        (c, ids[3], (own_first, own_second)),
        (1 - c, ids[5], (far_first, far_second)),
    ):
        for place, ref, m in merged(base, *refs):
            a, g, j = place // (2 * parts), (place // parts) % 2, place % parts
            start = where * hid + jnp.minimum(j * size, hid - size)
            out[a, g, pl.ds(pl.multiple_of(start, 16), size), :] = ref[m].astype(F32)


def wo_out_kernel(hid, ids, first, second, out):
    size, width = first.shape[1], first.shape[2]
    parts = first.shape[0] // 2
    per = 2 * width // 128
    for place, ref, m in merged(ids[5], first, second):
        l, a, j = place // (2 * parts), (place // parts) % 2, place % parts
        row = a * hid + jnp.minimum(j * size, hid - size)
        split_lanes(out, row, l * (per // 2), size, per, ref[m])


def last_out_kernel(ids, own_first, own_second, far_first, far_second, qkv, wout):
    c = ids[1]
    size = own_first.shape[1]
    side = far_first.shape[2]
    width = side // 3
    per = 2 * width // 128
    for where, refs in ((c, (own_first, own_second)), (1 - c, (far_first, far_second))):
        for place, ref, m in merged(ids[3], *refs):
            row = place * size
            for s in range(3):
                value = ref[m, :, s * width : (s + 1) * width]
                split_lanes(
                    qkv, row, s * per + where * (per // 2), size, 3 * per, value
                )
            if ref.shape[2] > side:
                split_lanes(wout, row, 0, size, per, ref[m, :, side:])


def stream(kept, sent, order, cross):
    index = lax.axis_index("dp")
    for bit, after in zip(order, order[1:]):
        got = yield sent, bit
        mine = lax.bitwise_and(index, after) != 0
        half = kept.shape[0] // 2
        ks, gs = (kept[:half], kept[half:]), (got[:half], got[half:])
        low, high = [(k.astype(F32) + g.astype(F32)).astype(BF) for k, g in zip(ks, gs)]
        sent = jnp.where(mine, low, high)
        kept = jnp.where(mine, high, low)
    got = yield sent, order[-1]
    value = (kept.astype(F32) + got.astype(F32)).astype(BF)
    if cross:
        value = yield value, "col"
    for bit in order[:0:-1]:
        got = yield value, bit
        value = jnp.concatenate([value, got], axis=0)
    got = yield value, order[0]
    return value, got


def small_stream(value, order):
    for bit in order:
        got = yield value, bit
        value = value + got
    return value


def group_sum(kept, sent):
    half = (kept + swap(sent, "row").astype(F32)).astype(BF)
    got = yield half, "col"
    half = (half.astype(F32) + got.astype(F32)).astype(BF)
    return half, swap(half, "row")


def group_steps(kept, sent):
    got = yield sent, "row"
    half = (kept + got.astype(F32)).astype(BF)
    got = yield half, "col"
    half = (half.astype(F32) + got.astype(F32)).astype(BF)
    got = yield half, "row"
    return half, got


class Streams:
    def __init__(self):
        self.work, self.flight, self.done, self.token = {}, {}, {}, None

    def step(self, name, got):
        try:
            value, way = self.work[name].send(got)
        except StopIteration as end:
            self.done[name] = end.value
            self.token = jax.tree.leaves(end.value)[0]
            return
        self.token = value
        self.flight[name] = swap(value, way) if isinstance(way, str) else dp_swap(value, way)

    def add(self, name, steps):
        self.work[name] = steps
        self.step(name, None)

    def run(self, names):
        for name in names:
            self.step(name, self.after(self.flight.pop(name)))

    def after(self, value):
        return lax.optimization_barrier((value, self.token))[0]


def place_of(order):
    index = lax.axis_index("dp").astype(jnp.int32)
    place = jnp.int32(0)
    for bit in order:
        place = 2 * place + (lax.bitwise_and(index, bit) != 0).astype(jnp.int32)
    return place


def shards(hidden_in, doc_lens, norm1_gain, wqkv, wout, norm2_gain, wi, wo, out_grad):
    tokens, _, width = hidden_in.shape
    half, full = 2 * width, 4 * width
    hid = wo.shape[1]
    count = lax.axis_size("dp")
    row, col = lax.axis_index("row"), lax.axis_index("col")
    side = lax.bitwise_and(lax.axis_index("dp"), 1)
    order = bits_of(count)
    ends = jnp.cumsum(doc_lens[0])
    other = order[1:2] + order[:1] + order[2:]
    bit = (lax.bitwise_and(lax.axis_index("dp"), other[0]) != 0).astype(jnp.int32)
    head = [row, col, side, place_of(order), bit, place_of(other)]
    ids = jnp.concatenate([jnp.stack([h.astype(jnp.int32) for h in head]), ends])

    places = jnp.arange(tokens, dtype=jnp.int32)
    passed = ends[None, :] <= places[:, None]
    doc_start = jnp.sum(jnp.where(passed, doc_lens[0][None, :], 0), axis=1)
    occupied = (places < ends[-1]).astype(BF)[:, None]
    frequency = jnp.exp(
        jnp.arange(HD // 2, dtype=F32) * (-2.0 * math.log(ROPE_BASE) / HD)
    )
    angles = (places - doc_start).astype(F32)[:, None] * jnp.tile(frequency, 4)[None, :]
    cosine, sine = jnp.cos(angles), jnp.sin(angles)

    own = hidden_in[:, 0, :]
    own_x = swap(own, "col")
    gains = jnp.concatenate([norm1_gain, norm2_gain], axis=0)
    gains, own_x = lax.optimization_barrier((gains, own_x))
    others = swap(jnp.stack([own, own_x]), "row")
    gains = ordered(col, gains, swap(gains, "col"), 1)
    gains = ordered(row, gains, swap(gains, "row"), 1)
    gain_one, gain_two = gains[0:1], gains[1:2]

    w_qkv = wqkv.transpose(0, 2, 3, 1, 4).reshape(2, 3, width, half)
    qkv_send = lax.dynamic_slice(
        w_qkv, (side, 0, 0, (1 - col) * width), (1, 3, width, width)
    )[0]
    qkv_y = swap(qkv_send, "col")
    qkv_n = dp_swap(qkv_y, 1)
    w_in = wi.transpose(0, 2, 3, 4, 1).reshape(2, 2, 2 * hid, width)
    in_send = lax.dynamic_slice(
        w_in, (side, 0, (1 - col) * hid, 0), (1, 2, hid, width)
    )[0]
    grad_own = out_grad[:, 0, :]
    in_send, grad_own, qkv_y = lax.optimization_barrier((in_send, grad_own, qkv_y))
    in_y = swap(in_send, "col")
    w_down = wo.reshape(2, hid, half)
    down_got = swap(lax.dynamic_index_in_dim(w_down, 1 - row, 0, False), "row")
    w_out = wout.reshape(2, width, half)
    out_got = swap(lax.dynamic_index_in_dim(w_out, 1 - row, 0, False), "row")

    qkv_n, down_got, out_got, occupied = lax.optimization_barrier(
        (qkv_n, down_got, out_got, occupied)
    )

    grad_x = swap(grad_own, "col")

    hidden, normed_one = call(
        norm_kernel,
        (((tokens, full), BF), ((tokens, full), BF)),
        ids, own, own_x, others, gain_one,
    )
    qkv, attended, probs = call(
        attend_kernel,
        (((tokens, 3 * width), BF), ((tokens, width), BF), ((width // HD, tokens, tokens), BF)),
        ids, normed_one, w_qkv, qkv_y, qkv_n, cosine, sine,
    )
    attended, in_y, grad_x = lax.optimization_barrier((attended, in_y, grad_x))
    in_n = dp_swap(in_y, 1)
    grad_half = ordered(col, grad_own, grad_x, 1) * occupied
    grad_other = swap(grad_half, "row")
    attended_got = swap(attended, "row")
    (branch,) = call(
        branch_kernel, (((tokens, half), BF),), ids, attended, attended_got, w_out,
    )
    branch = (branch.astype(F32) + swap(branch, "col").astype(F32)).astype(BF)
    branch_got = swap(branch, "row")

    wide = -(-hid // 128) * 128
    middle, normed_two, activated, mix = call(
        ffn_kernel,
        (
            ((tokens, full), F32), ((tokens, full), BF), ((tokens, wide), BF),
            ((2, tokens, hid), BF),
        ),
        ids, hidden, branch, branch_got, gain_two, w_in, in_y, in_n, grad_half, grad_other,
        w_down, down_got,
    )
    parts = max(count // 4, 1)
    size, _ = pieces(hid, parts)
    streams = Streams()
    blocks = (count // 2, size, width)
    kept, sent = call(
        ffn_back_kernel,
        (((tokens, half), F32), ((tokens, half), BF)),
        ids, mix, w_in, in_y, in_n,
        scratch=[pltpu.VMEM((2, tokens, half), F32)],
    )
    mix, sent = lax.optimization_barrier((mix, sent))
    halves = [
        part.reshape(blocks)
        for part in call(
            wi_kernel, (((2, parts, size, width), BF),) * 4, ids, mix, normed_two
        )
    ]
    streams.add("W1", stream(halves[0], halves[1], order, False))
    streams.add("C", group_sum(kept, sent))
    activated_got = swap(activated, "row")
    kept, sent = call(
        functools.partial(wo_kernel, hid), (((2, parts, size, width), BF),) * 2,
        ids, activated, streams.after(activated_got), grad_half,
    )
    streams.add("O", stream(kept.reshape(blocks), sent.reshape(blocks), other, False))
    streams.add("W2", stream(halves[2], halves[3], other, True))
    streams.run(["W1", "O", "C"])
    two_own, two_got = streams.done["C"]
    grad_middle, branch_grad, grad_attended, gain_two_grad = call(
        middle_back_kernel,
        (
            ((tokens, full), F32), ((tokens, half), BF), ((tokens, width), BF), ((1, full), F32),
        ),
        ids, two_own, two_got, middle, gain_two, grad_half, grad_other, w_out, out_got,
        scratch=[pltpu.VMEM((tokens, full), F32)],
    )
    (grad_proj,) = call(
        attend_back_kernel,
        (((tokens, 3 * width), BF),),
        ids, qkv, probs, grad_attended, cosine, sine,
    )
    rows = half // count
    near, far = (count // 2, rows, 3 * width + half), (count // 2, rows, 3 * width)
    halves = call(
        last_kernel, ((near, BF), (near, BF), (far, BF), (far, BF)),
        ids, normed_one, grad_proj, attended, attended_got, branch_grad,
    )
    streams.add("L2", stream(halves[2], halves[3], order, True))
    streams.add("L1", stream(halves[0], halves[1], order, False))
    kept, sent = call(
        qkv_back_kernel,
        (((tokens, half), F32), ((tokens, half), BF)),
        ids, streams.after(grad_proj), w_qkv, qkv_y, qkv_n,
        scratch=[pltpu.VMEM((2, tokens, half), F32)],
    )
    streams.add("D", group_steps(kept, sent))
    for _ in range(3):
        streams.run(["O", "W1", "W2", "L2", "L1", "D"])
    one_own, one_got = streams.done["D"]
    grad_in, gain_one_grad = call(
        input_back_kernel,
        (((tokens * width // 128, 128), F32), ((1, full), F32)),
        ids, one_own, one_got, hidden, gain_one, grad_middle,
        scratch=[pltpu.VMEM((tokens, full), F32)],
    )
    mine = 2 * row + col
    small = jnp.concatenate([pick(gain_one_grad, mine, 4, 1), pick(gain_two_grad, mine, 4, 1)])
    kept, sent = call(
        down_kernel,
        (((tokens, width), F32), ((tokens, width), BF)),
        ids, activated, streams.after(activated_got), w_down, middle,
    )
    hidden_out = (kept + swap(sent, "col").astype(F32)).astype(BF)
    streams.add("G", small_stream(small, order))
    if len(order) == 3:
        streams.run(LATE)
    else:
        for name in list(streams.flight):
            while name in streams.flight:
                streams.run([name])
    streams.run([name for name in ("O",) if name in streams.flight])
    (grad_wo,) = call(
        functools.partial(wo_out_kernel, hid), (((2 * hid * half // 128, 128), F32),),
        ids, *streams.done["O"],
        flops=8 * 10**9,
    )
    streams.token = grad_wo
    streams.run([name for name in ("W1", "W2") if name in streams.flight])
    (grad_wi,) = call(
        wi_out_kernel, (((2, 2, 2 * hid, width), F32),),
        ids, *streams.done["W1"], *streams.done["W2"],
        flops=8 * 10**9,
    )
    streams.token = grad_wi
    grad_wi = grad_wi.reshape(2, 2, 1, 2 * hid, width).transpose(0, 4, 1, 2, 3)
    streams.run([name for name in ("L1", "L2", "G") if name in streams.flight])
    grad_wqkv, grad_wout = call(
        last_out_kernel,
        (((half * 3 * half // 128, 128), F32), ((half * half // 128, 128), F32)),
        ids, *streams.done["L1"], *streams.done["L2"],
    )
    small = streams.done["G"]
    return (
        hidden_out[:, None, :],
        grad_in.reshape(tokens, 1, width),
        small[0:1],
        grad_wqkv.reshape(2, width, 3, 1, half),
        grad_wout.reshape(wout.shape),
        small[1:2],
        grad_wi,
        grad_wo.reshape(wo.shape),
    )


def solution(mesh):
    return jax.shard_map(
        shards,
        mesh=mesh,
        in_specs=(
            P("dp", "row", "col"),
            P("dp", None),
            P("row", "col"),
            P(None, "col", None, "row", None),
            P(None, "col", "row", None),
            P("row", "col"),
            P(None, "col", None, "row", None),
            P(None, "col", "row", None),
            P("dp", "row", "col"),
        ),
        out_specs=(
            P("dp", "row", "col"),
            P("dp", "row", "col"),
            P("row", "col"),
            P(None, "col", None, "row", None),
            P(None, "col", "row", None),
            P("row", "col"),
            P(None, "col", None, "row", None),
            P(None, "col", "row", None),
        ),
        check_vma=False,
    )
```
